256 devices in a mesh: seq: 64 (over z, x, core), head: 4 (over y).
Axes of the slice: x: 4, y: 4, z: 8, core: 2. Of those that a mesh axis runs over, the one named last changes fastest.
Arguments:
- queries: bfloat16 [32768, 6144], P('seq', 'head'), may hold values from -6 to 6
- key_rows: bfloat16 [32768, 6144], P('seq', 'head'), may hold values from -6 to 6
- values: bfloat16 [32768, 6144], P('seq', 'head'), may hold values from -6 to 6
- gate_input: bfloat16 [32768, 6144], P('seq', 'head'), may hold values from -6 to 6
- norm_gain: float32 [6144], P('head'), may hold values from 0.1 to 1.9
- out_weight: bfloat16 [6144, 6144], P('head', 'seq'), may hold values from -0.078125 to 0.078125
Outputs:
- projected: bfloat16 [32768, 6144], P(('seq', 'head'))
The draws below stay inside these ranges and needn't reach their ends.
All inputs are finite; a program needn't handle non-finite values.
Results may differ from the reference program's by a relative error of at most 0.02.
Values may be sent and summed in bfloat16 or wider, within the bound.
A program may use at most 192 MiB of HBM per device.

```python
import jax
import jax.numpy as jnp
from jax import lax

HEADS = 48
HEAD_DIM = 128
D = 6144
BLOCK = 512
TOK_DEV = 512
TOKENS = 32768
N_SEQ = 64
N_HEAD = 4


def level_of(own_key, dims, cuts, smallest, top_value):
    gain = 1.0
    for dim, blocks in cuts:
        steps = jax.random.uniform(jax.random.fold_in(jax.random.fold_in(own_key, 6), dim), (blocks,), jnp.float32, smallest / len(cuts), top_value / len(cuts))
        gain = gain * jnp.repeat(jnp.exp(steps), dims[dim] // blocks).reshape((-1,) + (1,) * (len(dims) - 1 - dim))
    return gain


def normal_values(key, shape, deviation, limit, cuts=(), held_as=jnp.bfloat16):
    values = deviation * jax.random.normal(key, shape, jnp.float32)
    if cuts:
        values = values * level_of(key, shape, cuts, -0.22, 0.18)
    return jnp.clip(values, -limit, limit).astype(held_as)


def setup_inputs(seed: int = 0) -> dict:
    arg_keys = jax.random.split(jax.random.key(seed), 7)
    return {
        "queries": normal_values(arg_keys[0], (TOKENS, D), 1.0, 6.0, ((0, 64), (1, 4))),
        "key_rows": normal_values(arg_keys[1], (TOKENS, D), 1.0, 6.0, ((0, 64), (1, 4))),
        "values": normal_values(arg_keys[2], (TOKENS, D), 1.0, 6.0, ((0, 64), (1, 4))),
        "gate_input": normal_values(arg_keys[3], (TOKENS, D), 1.0, 6.0, ((0, 64), (1, 4))),
        "norm_gain": jnp.clip(1.0 + 0.18 * jax.random.normal(arg_keys[4], (D,), jnp.float32), 0.1, 1.9),
        "out_weight": normal_values(arg_keys[5], (D, D), D ** -0.5, 0.078125, ((0, 4), (1, 64))),
    }


def head_attention(operands):
    query_head, key_head, value_head, gate_head, gain_head = operands
    causal = jnp.tril(jnp.ones((BLOCK, BLOCK), dtype=bool))
    count = TOKENS // BLOCK
    query_blocks = query_head.reshape(count, BLOCK, HEAD_DIM)
    key_blocks = key_head.reshape(count, BLOCK, HEAD_DIM)
    value_blocks = value_head.reshape(count, BLOCK, HEAD_DIM)

    def advance(state, block):
        query_blk, key_blk, value_blk = block
        inter = jnp.dot(query_blk.astype(jnp.float32), state, precision=lax.Precision.HIGHEST)
        scores = jnp.dot(query_blk, key_blk.T, preferred_element_type=jnp.float32)
        weights = jnp.where(causal, scores, 0.0).astype(jnp.bfloat16)
        intra = jnp.dot(weights, value_blk, preferred_element_type=jnp.float32)
        state = state + jnp.dot(key_blk.T, value_blk, preferred_element_type=jnp.float32)
        return (state, inter + intra)
    start_state = jnp.zeros((HEAD_DIM, HEAD_DIM), jnp.float32)
    final_state, attended = lax.scan(advance, start_state, (query_blocks, key_blocks, value_blocks))
    attended = attended.reshape(TOKENS, HEAD_DIM)
    mean_square = lax.optimization_barrier(jnp.mean(attended * attended, axis=-1, keepdims=True))
    gated = jax.nn.silu(gate_head.astype(jnp.float32))
    return (attended * lax.rsqrt(mean_square + 1e-06) * gain_head[None, :] * gated).astype(jnp.bfloat16)

def split_heads(array):
    return jnp.transpose(array.reshape(TOKENS, HEADS, HEAD_DIM), (1, 0, 2))

def reference(queries, key_rows, values, gate_input, norm_gain, out_weight):
    normed = lax.map(head_attention, (split_heads(queries), split_heads(key_rows), split_heads(values), split_heads(gate_input), norm_gain.reshape(HEADS, HEAD_DIM)))
    normed = jnp.transpose(normed, (1, 0, 2)).reshape(TOKENS, D)
    group_width = D // N_HEAD

    def project_rows(rows):
        total = jnp.zeros((rows.shape[0], D), jnp.float32)
        for group in range(N_HEAD):
            piece = jnp.dot(rows[:, group * group_width:(group + 1) * group_width], out_weight[group * group_width:(group + 1) * group_width], preferred_element_type=jnp.float32)
            total = total + lax.optimization_barrier(piece.astype(jnp.bfloat16)).astype(jnp.float32)
        return total.astype(jnp.bfloat16)
    projected = lax.map(project_rows, normed.reshape(N_SEQ, TOK_DEV, D))
    return projected.reshape(TOKENS, D)
```

```python
import functools

import jax
import jax.numpy as jnp
from jax import lax
from jax.experimental import pallas as pl
from jax.experimental.pallas import tpu as pltpu
from jax.sharding import PartitionSpec as P

HD = 128
NZ, NX, NC, NY = 8, 4, 2, 4
NP = NX * NC
TOK = 512
WID = 1536
HEADS = WID // HD
SH = 96
PLANE = NP * SH
D = NZ * PLANE
QT = TOK // NY
PIECE = WID // NP
SUB = PIECE // NZ
HALF = SH // 2
HC = PLANE // 2
F32, BF16 = jnp.float32, jnp.bfloat16
NT = (((1,), (1,)), ((), ()))
TN = (((0,), (0,)), ((), ()))


def kernel(
    q_hbm, k_hbm, v_hbm, g_hbm, gain_ref, w_hbm, o_hbm,
    qb, kb, vb, gb, wraw, wt, st, sin, intra, gate, nrm,
    pr1, pr3, zt, za, zb, zp, pf, t1, t2, r1, r2, ob,
    ld, out_sem, zs, zr, xs, xr, ss, sr, p1s, p1r, p2s, p2r, p3s, p3r, p4s, p4r, ys, yr,
):
    s = lax.axis_index("seq")
    h = lax.axis_index("head")
    c = lax.rem(s, NC)
    x = lax.rem(s // NC, NX)
    z = s // NP
    p = lax.rem(s, NP)

    def at_zx(zz, xx, cc):
        return (zz * NX + xx) * NC + cc

    zu, zd = lax.rem(z + 1, NZ), lax.rem(z + NZ - 1, NZ)
    xu, xd = lax.rem(x + 1, NX), lax.rem(x + NX - 1, NX)
    hu, hd, h2 = lax.rem(h + 1, NY), lax.rem(h + NY - 1, NY), lax.rem(h + 2, NY)
    dev_zu, dev_zd = at_zx(zu, x, c), at_zx(zd, x, c)
    dev_xu, dev_xd = at_zx(z, xu, c), at_zx(z, xd, c)
    dev_sib = at_zx(z, x, 1 - c)

    sends = []

    def remote(src, dst, send_sem, recv_sem, seq=s, head=h):
        return pltpu.make_async_remote_copy(
            src_ref=src, dst_ref=dst, send_sem=send_sem, recv_sem=recv_sem,
            device_id=(seq, head), device_id_type=pl.DeviceIdType.MESH,
        )

    def send(*args, **kw):
        cp = remote(*args, **kw)
        cp.start()
        sends.append(cp)

    def arrive(dst, recv_sem):
        remote(dst, dst, recv_sem, recv_sem, seq=dev_sib).wait_recv()

    def plane(j):
        off = -(j + 1) // 2 if j % 2 else j // 2
        return lax.rem(z + off + NZ, NZ)

    loads = [
        pltpu.make_async_copy(src, dst, ld.at[i])
        for i, (src, dst) in enumerate(
            ((k_hbm, kb), (v_hbm, vb), (w_hbm, wraw), (q_hbm, qb), (g_hbm, gb))
        )
    ]
    for cp in loads:
        cp.start()

    bar = pltpu.get_barrier_semaphore()
    for i in range(1, NP):
        pl.semaphore_signal(bar, inc=1, device_id=(z * NP + lax.rem(p + i, NP), h), device_id_type=pl.DeviceIdType.MESH)
    for i in range(1, NZ):
        pl.semaphore_signal(bar, inc=1, device_id=(lax.rem(z + i, NZ) * NP + p, h), device_id_type=pl.DeviceIdType.MESH)
    for hh in (hu, hd):
        pl.semaphore_signal(bar, inc=1, device_id=(s, hh), device_id_type=pl.DeviceIdType.MESH)

    def shard(pln, xx, cc):
        return wt.at[pln, xx, cc]

    def z_start():
        own = shard(z, x, c)
        send(own, own, zs.at[0], zr.at[1], seq=dev_zu)
        send(own, own, zs.at[1], zr.at[2], seq=dev_zd)

    def z_recv(j):
        ref = shard(plane(j), x, c)
        if j == 7:
            arrive(ref.at[pl.ds(0, HALF)], zr.at[7])
            arrive(ref.at[pl.ds(HALF, HALF)], zr.at[8])
            return
        arrive(ref, zr.at[j])
        to = dev_zu if j % 2 else dev_zd
        if j == 5:
            ref = ref.at[pl.ds(0, HALF)]
        if j == 6:
            ref = ref.at[pl.ds(HALF, HALF)]
        send(ref, ref, zs.at[j + 1], zr.at[j + 2], seq=to)

    def x_start(j):
        ref = shard(plane(j), x, c)
        send(ref, ref, xs.at[j, 0], xr.at[j, 0], seq=dev_xu)
        send(ref, ref, xs.at[j, 1], xr.at[j, 1], seq=dev_xd)

    def x_forward(j):
        pln = plane(j)
        ref = shard(pln, xd, c)
        arrive(ref, xr.at[j, 0])
        ref = ref.at[pl.ds(0, HALF)]
        send(ref, ref, xs.at[j, 2], xr.at[j, 2], seq=dev_xu)
        ref = shard(pln, xu, c)
        arrive(ref, xr.at[j, 1])
        ref = ref.at[pl.ds(HALF, HALF)]
        send(ref, ref, xs.at[j, 3], xr.at[j, 3], seq=dev_xd)

    def sib_start(j):
        pln = plane(j)
        ref = shard(pln, lax.rem(x + 2, NX), c)
        arrive(ref.at[pl.ds(0, HALF)], xr.at[j, 2])
        arrive(ref.at[pl.ds(HALF, HALF)], xr.at[j, 3])
        for i in range(NX):
            ref = shard(pln, i, c)
            send(ref, ref, ss.at[j, i], sr.at[j, i], seq=dev_sib)

    def sib_recv(j):
        pln = plane(j)
        for i in range(NX):
            arrive(shard(pln, i, 1 - c), sr.at[j, i])

    with jax.named_scope("local_state"):
        loads[0].wait()
        loads[1].wait()

        def one_state(i, carry):
            cols = pl.ds(pl.multiple_of(i * HD, HD), HD)
            st[cols, :] = lax.dot_general(kb[:, cols], vb[:, cols], TN, preferred_element_type=F32).astype(BF16)
            return carry

        lax.fori_loop(0, HEADS, one_state, 0)

    with jax.named_scope("entry_barrier"):
        pl.semaphore_wait(bar, NP - 1 + NZ - 1 + 2)

    def piece_rows(i):
        return pl.ds(pl.multiple_of(i * PIECE, PIECE), PIECE)

    with jax.named_scope("plane_send"):
        for i in range(1, NP):
            to = lax.rem(p + i, NP)
            send(st.at[piece_rows(to)], pr1.at[p], p1s.at[i], p1r.at[i], seq=z * NP + to)
        pr1[p] = st[piece_rows(p), :]

    with jax.named_scope("weight_transpose"):
        loads[2].wait()
        eye = (lax.broadcasted_iota(jnp.int32, (SH, SH), 0) == lax.broadcasted_iota(jnp.int32, (SH, SH), 1)).astype(BF16)
        wt[z, x, c] = lax.dot_general(eye, wraw[...], NT, preferred_element_type=F32).astype(BF16)
        z_start()

    loads[3].wait()
    HB = TOK // 2
    tri = lax.broadcasted_iota(jnp.int32, (HB, HB), 0) >= lax.broadcasted_iota(jnp.int32, (HB, HB), 1)

    def one_intra(i, carry):
        cols = pl.ds(pl.multiple_of(i * HD, HD), HD)
        lo, hi = pl.ds(0, HB), pl.ds(HB, HB)
        v_lo = vb[lo, cols]
        sc = lax.dot_general(qb[lo, cols], kb[lo, cols], NT, preferred_element_type=F32)
        sc = jnp.where(tri, sc, 0.0).astype(BF16)
        intra[lo, cols] = jnp.dot(sc, v_lo, preferred_element_type=F32)
        sa = lax.dot_general(qb[hi, cols], kb[lo, cols], NT, preferred_element_type=F32).astype(BF16)
        sd = lax.dot_general(qb[hi, cols], kb[hi, cols], NT, preferred_element_type=F32)
        sd = jnp.where(tri, sd, 0.0).astype(BF16)
        intra[hi, cols] = jnp.dot(sa, v_lo, preferred_element_type=F32) + jnp.dot(sd, vb[hi, cols], preferred_element_type=F32)
        return carry

    def one_gate(i, carry):
        cols = pl.ds(pl.multiple_of(i * HD, HD), HD)
        gi = gb[:, cols].astype(F32)
        gate[:, cols] = gi / (1.0 + jnp.exp(-gi)) * gain_ref[:, cols]
        return carry

    with jax.named_scope("intra_a"):
        lax.fori_loop(0, HEADS // 2, one_intra, 0)

    def sub_rows(i):
        return pl.ds(pl.multiple_of(i * SUB, SUB), SUB)

    with jax.named_scope("plane_recv"):
        for i in range(1, NP):
            arrive(pr1.at[lax.rem(p + NP - i, NP)], p1r.at[i])
        total = pr1[0].astype(F32)
        for i in range(1, NP):
            total = total + pr1[i].astype(F32)
        zt[...] = total
        for i in range(1, NZ):
            to = lax.rem(z + i, NZ)
            send(zt.at[sub_rows(to)], za.at[z], p2s.at[i], p2r.at[i], seq=to * NP + p)
        za[z] = zt[sub_rows(z), :]
        x_start(0)

    with jax.named_scope("intra_b"):
        lax.fori_loop(HEADS // 2, HEADS, one_intra, 0)

    with jax.named_scope("z_scan"):
        for i in range(1, NZ):
            arrive(za.at[lax.rem(z + NZ - i, NZ)], p2r.at[i])
        run = jnp.zeros((SUB, HD), F32)
        for i in range(NZ):
            zb[i] = run
            run = run + za[i]
        for i in range(1, NZ):
            to = lax.rem(z + i, NZ)
            send(zb.at[to], zp.at[sub_rows(z)], p3s.at[i], p3r.at[i], seq=to * NP + p)
        zp[sub_rows(z), :] = zb[z]

    with jax.named_scope("gate"):
        loads[4].wait()
        lax.fori_loop(0, HEADS, one_gate, 0)

    with jax.named_scope("z_back"):
        for i in range(1, NZ):
            arrive(zp.at[sub_rows(lax.rem(z + NZ - i, NZ))], p3r.at[i])
        run = zp[...]
        for i in range(NP):
            pr3[i] = run.astype(BF16)
            run = run + pr1[i].astype(F32)
        for i in range(1, NP):
            to = lax.rem(p + i, NP)
            send(pr3.at[to], sin.at[piece_rows(p)], p4s.at[i], p4r.at[i], seq=z * NP + to)
        sin[piece_rows(p), :] = pr3[p]

    with jax.named_scope("gather_early"):
        x_forward(0)
        z_recv(1)
        z_recv(2)
        x_start(1)
        z_recv(3)
        z_recv(4)
        sib_start(0)

    with jax.named_scope("state_recv"):
        for i in range(1, NP):
            arrive(sin.at[piece_rows(lax.rem(p + NP - i, NP))], p4r.at[i])

    def one_head(i, carry):
        cols = pl.ds(pl.multiple_of(i * HD, HD), HD)
        att = intra[:, cols] + jnp.dot(qb[:, cols], sin[cols, :], preferred_element_type=F32)
        ms = jnp.mean(att * att, axis=-1, keepdims=True)
        nrm[:, cols] = (att * lax.rsqrt(ms + 1e-06) * gate[:, cols]).astype(BF16)
        return carry

    with jax.named_scope("attend"):
        lax.fori_loop(0, HEADS, one_head, 0)

    def q_rows(i):
        return pl.ds(pl.multiple_of(i * QT, QT), QT)

    def project(j):
        pln = plane(j)
        for i in range(NX):
            w = wt[pln, i].reshape(NC * SH, WID)
            pf[j % 3, :, pl.ds(i * NC * SH, NC * SH)] = lax.dot_general(nrm[...], w, NT, preferred_element_type=F32)

    def rs_first(j):
        t1[j, 0] = pf[j % 3, q_rows(h2), pl.ds(0, HC)].astype(BF16)
        t1[j, 1] = pf[j % 3, q_rows(h2), pl.ds(HC, HC)].astype(BF16)
        send(t1.at[j, 0], r1.at[j, 0], ys.at[j, 0], yr.at[j, 0], head=hu)
        send(t1.at[j, 1], r1.at[j, 1], ys.at[j, 1], yr.at[j, 1], head=hd)

    def rs_second(j):
        a = j % 3
        t2[j, 0, :, pl.ds(HC, HC)] = pf[a, q_rows(hu), pl.ds(HC, HC)].astype(BF16)
        t2[j, 1, :, pl.ds(0, HC)] = pf[a, q_rows(hd), pl.ds(0, HC)].astype(BF16)
        arrive(r1.at[j, 0], yr.at[j, 0])
        t2[j, 0, :, pl.ds(0, HC)] = (pf[a, q_rows(hu), pl.ds(0, HC)] + r1[j, 0].astype(F32)).astype(BF16)
        send(t2.at[j, 0], r2.at[j, 0], ys.at[j, 2], yr.at[j, 2], head=hu)
        arrive(r1.at[j, 1], yr.at[j, 1])
        t2[j, 1, :, pl.ds(HC, HC)] = (pf[a, q_rows(hd), pl.ds(HC, HC)] + r1[j, 1].astype(F32)).astype(BF16)
        send(t2.at[j, 1], r2.at[j, 1], ys.at[j, 3], yr.at[j, 3], head=hd)

    outs = []

    def rs_last(j):
        arrive(r2.at[j, 0], yr.at[j, 2])
        arrive(r2.at[j, 1], yr.at[j, 3])
        ob[j] = (pf[j % 3, q_rows(h), :] + r2[j, 0].astype(F32) + r2[j, 1].astype(F32)).astype(BF16)
        cols = pl.ds(pl.multiple_of(plane(j) * PLANE, PLANE), PLANE)
        cp = pltpu.make_async_copy(ob.at[j], o_hbm.at[:, cols], out_sem.at[j])
        cp.start()
        outs.append(cp)

    for j in range(NZ + 2):
        if j < NZ:
            with jax.named_scope(f"plane_wait_{j}"):
                sib_recv(j)
            with jax.named_scope(f"project_{j}"):
                project(j)
                rs_first(j)
        if j + 1 < NZ:
            with jax.named_scope(f"gather_{j}"):
                x_forward(j + 1)
                if j + 2 < NZ:
                    x_start(j + 2)
                if j == 0:
                    z_recv(5)
                    z_recv(6)
                if j == 1:
                    z_recv(7)
        if 1 <= j <= NZ:
            with jax.named_scope(f"reduce_{j}"):
                rs_second(j - 1)
        if j + 1 < NZ:
            with jax.named_scope(f"sibling_{j}"):
                sib_start(j + 1)
        if j >= 2:
            with jax.named_scope(f"finish_{j}"):
                rs_last(j - 2)

    with jax.named_scope("drain"):
        for cp in outs:
            cp.wait()
        for cp in sends:
            cp.wait_send()


def per_device(queries, key_rows, values, gate_input, norm_gain, out_weight):
    anyspec = pl.BlockSpec(memory_space=pl.ANY)
    dma = lambda *n: pltpu.SemaphoreType.DMA(n)
    return pl.pallas_call(
        kernel,
        out_shape=jax.ShapeDtypeStruct((QT, D), BF16),
        in_specs=[anyspec] * 4 + [pl.BlockSpec(memory_space=pltpu.VMEM), anyspec],
        out_specs=anyspec,
        scratch_shapes=[
            pltpu.VMEM((TOK, WID), BF16),
            pltpu.VMEM((TOK, WID), BF16),
            pltpu.VMEM((TOK, WID), BF16),
            pltpu.VMEM((TOK, WID), BF16),
            pltpu.VMEM((WID, SH), BF16),
            pltpu.VMEM((NZ, NX, NC, SH, WID), BF16),
            pltpu.VMEM((WID, HD), BF16),
            pltpu.VMEM((WID, HD), BF16),
            pltpu.VMEM((TOK, WID), F32),
            pltpu.VMEM((TOK, WID), F32),
            pltpu.VMEM((TOK, WID), BF16),
            pltpu.VMEM((NP, PIECE, HD), BF16),
            pltpu.VMEM((NP, PIECE, HD), BF16),
            pltpu.VMEM((PIECE, HD), F32),
            pltpu.VMEM((NZ, SUB, HD), F32),
            pltpu.VMEM((NZ, SUB, HD), F32),
            pltpu.VMEM((PIECE, HD), F32),
            pltpu.VMEM((3, TOK, PLANE), F32),
            pltpu.VMEM((NZ, 2, QT, HC), BF16),
            pltpu.VMEM((NZ, 2, QT, PLANE), BF16),
            pltpu.VMEM((NZ, 2, QT, HC), BF16),
            pltpu.VMEM((NZ, 2, QT, PLANE), BF16),
            pltpu.VMEM((NZ, QT, PLANE), BF16),
            dma(5), dma(NZ),
            dma(9), dma(9),
            dma(NZ, 4), dma(NZ, 4),
            dma(NZ, NX), dma(NZ, NX),
            dma(NP), dma(NP), dma(NZ), dma(NZ), dma(NZ), dma(NZ), dma(NP), dma(NP),
            dma(NZ, 4), dma(NZ, 4),
        ],
        compiler_params=pltpu.CompilerParams(
            collective_id=0, has_side_effects=True, vmem_limit_bytes=60 * 1024 * 1024
        ),
    )(queries, key_rows, values, gate_input, norm_gain.reshape(1, WID), out_weight)


def solution(mesh):
    in_specs = (
        P("seq", "head"),
        P("seq", "head"),
        P("seq", "head"),
        P("seq", "head"),
        P("head"),
        P("head", "seq"),
    )
    return jax.shard_map(
        per_device,
        mesh=mesh,
        in_specs=in_specs,
        out_specs=P(("seq", "head"), None),
        check_vma=False,
    )
```

```python
import functools

import jax
import jax.numpy as jnp
from jax import lax
from jax.experimental import pallas as pl
from jax.experimental.pallas import tpu as pltpu
from jax.sharding import PartitionSpec as P

HD = 128
NZ, NX, NC, NY = 8, 4, 2, 4
NP = NX * NC
TOK = 512
WID = 1536
HEADS = WID // HD
SH = 96
PLANE = NP * SH
D = NZ * PLANE
QT = TOK // NY
PIECE = WID // NP
SUB = PIECE // NZ
HALF = SH // 2
PARTS = 2
SPLIT = 8
NCH = NZ * PARTS
CW = PLANE // PARTS
QH = QT // 2
F32, BF16 = jnp.float32, jnp.bfloat16
KINDS = "BAABBBBA"
ORDER = (0, 4, 1, 2, 6, 3, 5, 7)
PLAN = {
    "intra_a": "O0",
    "plane_recv": "X0",
    "intra_b": "Z2 Z1",
    "z_sum": "F0",
    "gate": "Z4 X4",
    "z_back": "S0 A0",
    "back_sum": "Z3",
    "state_recv": "F4 Z6 X6",
    "chunk_1": "S4 X3",
    "after_2": "S1 F6",
    "after_4": "Z5 S2 X5",
    "after_5": "F3",
    "after_6": "S6",
    "chunk_7": "Z7 A6",
    "after_7": "F5",
    "after_8": "S3",
    "after_9": "S5 A5",
    "after_12": "S7",
}
NT = (((1,), (1,)), ((), ()))
TN = (((0,), (0,)), ((), ()))


def kernel(
    q_hbm, k_hbm, v_hbm, g_hbm, gain_ref, w_hbm, o_hbm,
    qb, kb, vb, gb, wt, st, sin, intra, gate, nrm,
    pr1, pr3, zt, za, zb, zp, pf, t1, t2, r1, r2, ob,
    ld, out_sem, zs, zr, xs, xr, fs, fr, ss, sr, p1s, p1r, p2s, p2r, p3s, p3r, p4s, p4r, ys, yr,
):
    s = lax.axis_index("seq")
    h = lax.axis_index("head")
    c = lax.rem(s, NC)
    x = lax.rem(s // NC, NX)
    z = s // NP
    p = lax.rem(s, NP)

    def at_zx(zz, xx, cc):
        return (zz * NX + xx) * NC + cc

    zu, zd = lax.rem(z + 1, NZ), lax.rem(z + NZ - 1, NZ)
    xu, xd = lax.rem(x + 1, NX), lax.rem(x + NX - 1, NX)
    hu, hd, h2 = lax.rem(h + 1, NY), lax.rem(h + NY - 1, NY), lax.rem(h + 2, NY)
    dev_zu, dev_zd = at_zx(zu, x, c), at_zx(zd, x, c)
    dev_xu, dev_xd = at_zx(z, xu, c), at_zx(z, xd, c)
    dev_sib = at_zx(z, x, 1 - c)

    sends = []

    def remote(src, dst, send_sem, recv_sem, seq=s, head=h):
        return pltpu.make_async_remote_copy(
            src_ref=src, dst_ref=dst, send_sem=send_sem, recv_sem=recv_sem,
            device_id=(seq, head), device_id_type=pl.DeviceIdType.MESH,
        )

    def send(*args, **kw):
        cp = remote(*args, **kw)
        cp.start()
        sends.append(cp)

    def arrive(dst, recv_sem):
        remote(dst, dst, recv_sem, recv_sem, seq=dev_sib).wait_recv()

    def plane(j):
        off = -(j + 1) // 2 if j % 2 else j // 2
        return lax.rem(z + off + NZ, NZ)

    loads = [
        pltpu.make_async_copy(src, dst, ld.at[i])
        for i, (src, dst) in enumerate(
            ((k_hbm, kb), (v_hbm, vb), (w_hbm, wt.at[z, x, c]), (q_hbm, qb), (g_hbm, gb))
        )
    ]
    for cp in loads:
        cp.start()

    bar = pltpu.get_barrier_semaphore()
    for i in range(1, NP):
        pl.semaphore_signal(bar, inc=1, device_id=(z * NP + lax.rem(p + i, NP), h), device_id_type=pl.DeviceIdType.MESH)
    for i in range(1, NZ):
        pl.semaphore_signal(bar, inc=1, device_id=(lax.rem(z + i, NZ) * NP + p, h), device_id_type=pl.DeviceIdType.MESH)
    for hh in (hu, hd):
        pl.semaphore_signal(bar, inc=1, device_id=(s, hh), device_id_type=pl.DeviceIdType.MESH)

    def shard(pln, xx, cc):
        return wt.at[pln, xx, cc]

    def z_start():
        own = shard(z, x, c)
        send(own, own, zs.at[0], zr.at[1], seq=dev_zu)
        send(own, own, zs.at[1], zr.at[2], seq=dev_zd)

    def z_recv(j):
        ref = shard(plane(j), x, c)
        if j == 7:
            arrive(ref.at[pl.ds(0, HALF)], zr.at[7])
            arrive(ref.at[pl.ds(HALF, HALF)], zr.at[8])
            return
        arrive(ref, zr.at[j])
        to = dev_zu if j % 2 else dev_zd
        if j == 5:
            ref = ref.at[pl.ds(0, HALF)]
        if j == 6:
            ref = ref.at[pl.ds(HALF, HALF)]
        send(ref, ref, zs.at[j + 1], zr.at[j + 2], seq=to)

    def sib_send(j, i):
        ref = shard(plane(j), lax.rem(x + i, NX), c)
        send(ref, ref, ss.at[j, i], sr.at[j, i], seq=dev_sib)

    def x_start(j):
        ref = shard(plane(j), x, c)
        send(ref, ref, xs.at[j, 0], xr.at[j, 0], seq=dev_xu)
        send(ref, ref, xs.at[j, 1], xr.at[j, 1], seq=dev_xd)
        sib_send(j, 0)

    def x_forward(j):
        pln = plane(j)
        ref = shard(pln, xd, c)
        arrive(ref, xr.at[j, 0])
        ref = ref.at[pl.ds(0, HALF)]
        send(ref, ref, xs.at[j, 2], xr.at[j, 2], seq=dev_xu)
        sib_send(j, NX - 1)
        ref = shard(pln, xu, c)
        arrive(ref, xr.at[j, 1])
        ref = ref.at[pl.ds(HALF, HALF)]
        send(ref, ref, xs.at[j, 3], xr.at[j, 3], seq=dev_xd)
        sib_send(j, 1)

    def halves(ref):
        return ref.at[pl.ds(0, HALF)], ref.at[pl.ds(HALF, HALF)]

    def whole_start(j):
        for i in range(1, NX):
            ref = shard(plane(j), lax.rem(x + i, NX), c)
            if j % 2 or j == 0:
                up = halves(ref)[0] if j == 5 else ref
                send(up, up, fs.at[j + 2 - (j == 0), i], fr.at[j + 2 - (j == 0), i], seq=dev_zu)
            if j % 2 == 0:
                dn = halves(ref)[1] if j == 6 else ref
                send(dn, dn, fs.at[j + 2, i], fr.at[j + 2, i], seq=dev_zd)

    def fill(j):
        pln = plane(j)
        if KINDS[j] == "B":
            lo, hi = halves(shard(pln, lax.rem(x + 2, NX), c))
            arrive(lo, xr.at[j, 2])
            arrive(hi, xr.at[j, 3])
            sib_send(j, 2)
            return
        sib_send(j, 0)
        for i in range(1, NX):
            ref = shard(pln, lax.rem(x + i, NX), c)
            if j == 7:
                lo, hi = halves(ref)
                arrive(lo, fr.at[7, i])
                arrive(hi, fr.at[8, i])
            else:
                arrive(ref, fr.at[j, i])
            sib_send(j, i)

    def sib_recv(j):
        for i in range(NX):
            arrive(shard(plane(j), lax.rem(x + i, NX), 1 - c), sr.at[j, i])

    stages = {"O": lambda j: z_start(), "Z": z_recv, "X": x_start, "F": x_forward, "A": whole_start, "S": fill}

    def gather(at):
        for name in PLAN.get(at, "").split():
            with jax.named_scope(f"gather_{name}"):
                stages[name[0]](int(name[1]))

    with jax.named_scope("local_state"):
        loads[0].wait()
        loads[1].wait()

        def one_state(i, carry):
            cols = pl.ds(pl.multiple_of(i * HD, HD), HD)
            st[cols, :] = lax.dot_general(kb[:, cols], vb[:, cols], TN, preferred_element_type=F32).astype(BF16)
            return carry

        lax.fori_loop(0, HEADS, one_state, 0)

    with jax.named_scope("entry_barrier"):
        pl.semaphore_wait(bar, NP - 1 + NZ - 1 + 2)

    def piece_rows(i):
        return pl.ds(pl.multiple_of(i * PIECE, PIECE), PIECE)

    with jax.named_scope("plane_send"):
        for i in range(1, NP):
            to = lax.rem(p + i, NP)
            send(st.at[piece_rows(to)], pr1.at[p], p1s.at[i], p1r.at[i], seq=z * NP + to)
        pr1[p] = st[piece_rows(p), :]

    with jax.named_scope("weight_send"):
        loads[2].wait()
        gather("intra_a")

    loads[3].wait()
    HB = TOK // 2
    tri = lax.broadcasted_iota(jnp.int32, (HB, HB), 0) >= lax.broadcasted_iota(jnp.int32, (HB, HB), 1)

    def one_intra(i, carry):
        cols = pl.ds(pl.multiple_of(i * HD, HD), HD)
        lo, hi = pl.ds(0, HB), pl.ds(HB, HB)
        v_lo = vb[lo, cols]
        sc = lax.dot_general(qb[lo, cols], kb[lo, cols], NT, preferred_element_type=F32)
        sc = jnp.where(tri, sc, 0.0).astype(BF16)
        intra[lo, cols] = jnp.dot(sc, v_lo, preferred_element_type=F32)
        sa = lax.dot_general(qb[hi, cols], kb[lo, cols], NT, preferred_element_type=F32).astype(BF16)
        sd = lax.dot_general(qb[hi, cols], kb[hi, cols], NT, preferred_element_type=F32)
        sd = jnp.where(tri, sd, 0.0).astype(BF16)
        intra[hi, cols] = jnp.dot(sa, v_lo, preferred_element_type=F32) + jnp.dot(sd, vb[hi, cols], preferred_element_type=F32)
        return carry

    def one_gate(i, carry):
        cols = pl.ds(pl.multiple_of(i * HD, HD), HD)
        gi = gb[:, cols].astype(F32)
        gate[:, cols] = gi / (1.0 + jnp.exp(-gi)) * gain_ref[cols].reshape(1, HD)
        return carry

    with jax.named_scope("intra_a"):
        lax.fori_loop(0, SPLIT, one_intra, 0)

    def sub_rows(i):
        return pl.ds(pl.multiple_of(i * SUB, SUB), SUB)

    gather("plane_recv")
    with jax.named_scope("plane_recv"):
        for i in range(1, NP):
            arrive(pr1.at[lax.rem(p + NP - i, NP)], p1r.at[i])
        gather("plane_sum")
        total = pr1[0].astype(F32)
        for i in range(1, NP):
            total = total + pr1[i].astype(F32)
        zt[...] = total
        for i in range(1, NZ):
            to = lax.rem(z + i, NZ)
            send(zt.at[sub_rows(to)], za.at[z], p2s.at[i], p2r.at[i], seq=to * NP + p)
        za[z] = zt[sub_rows(z), :]

    gather("intra_b")
    with jax.named_scope("intra_b"):
        lax.fori_loop(SPLIT, HEADS, one_intra, 0)

    gather("z_scan")
    with jax.named_scope("z_scan"):
        for i in range(1, NZ):
            arrive(za.at[lax.rem(z + NZ - i, NZ)], p2r.at[i])
        gather("z_sum")
        run = jnp.zeros((SUB, HD), F32)
        for i in range(NZ):
            zb[i] = run
            run = run + za[i]
        for i in range(1, NZ):
            to = lax.rem(z + i, NZ)
            send(zb.at[to], zp.at[sub_rows(z)], p3s.at[i], p3r.at[i], seq=to * NP + p)
        zp[sub_rows(z), :] = zb[z]

    gather("gate")
    with jax.named_scope("gate"):
        loads[4].wait()
        lax.fori_loop(0, HEADS, one_gate, 0)

    gather("z_back")
    with jax.named_scope("z_back"):
        for i in range(1, NZ):
            arrive(zp.at[sub_rows(lax.rem(z + NZ - i, NZ))], p3r.at[i])
        gather("back_sum")
        run = zp[...]
        for i in range(NP):
            pr3[i] = run.astype(BF16)
            run = run + pr1[i].astype(F32)
        for i in range(1, NP):
            to = lax.rem(p + i, NP)
            send(pr3.at[to], sin.at[piece_rows(p)], p4s.at[i], p4r.at[i], seq=z * NP + to)
        sin[piece_rows(p), :] = pr3[p]

    gather("state_recv")
    with jax.named_scope("state_recv"):
        for i in range(1, NP):
            arrive(sin.at[piece_rows(lax.rem(p + NP - i, NP))], p4r.at[i])

    def one_head(i, carry):
        cols = pl.ds(pl.multiple_of(i * HD, HD), HD)
        att = intra[:, cols] + jnp.dot(qb[:, cols], sin[cols, :], preferred_element_type=F32)
        ms = jnp.mean(att * att, axis=-1, keepdims=True)
        nrm[:, cols] = (att * lax.rsqrt(ms + 1e-06) * gate[:, cols]).astype(BF16)
        return carry

    gather("attend")
    with jax.named_scope("attend"):
        lax.fori_loop(0, HEADS, one_head, 0)

    def q_rows(i):
        return pl.ds(pl.multiple_of(i * QT, QT), QT)

    def project(n):
        w = wt[plane(ORDER[n // PARTS]), pl.ds(n % PARTS * (NX // PARTS), NX // PARTS)].reshape(CW, WID)
        pf[n % 3] = lax.dot_general(nrm[...], w, NT, preferred_element_type=F32)

    def half_rows(i, half):
        return pl.ds(pl.multiple_of(i * QT + half * QH, QH), QH)

    def rs_first(n):
        for half, to in ((0, hu), (1, hd)):
            t1[n, half] = pf[n % 3, half_rows(h2, half), :].astype(BF16)
            send(t1.at[n, half], r1.at[n, half], ys.at[n, half], yr.at[n, half], head=to)

    def rs_second(n):
        for half, to in ((0, hu), (1, hd)):
            same, other = pl.ds(half * QH, QH), pl.ds((1 - half) * QH, QH)
            t2[n, half, other, :] = pf[n % 3, half_rows(to, 1 - half), :].astype(BF16)
            arrive(r1.at[n, half], yr.at[n, half])
            t2[n, half, same, :] = (pf[n % 3, half_rows(to, half), :] + r1[n, half].astype(F32)).astype(BF16)
            send(t2.at[n, half], r2.at[n, half], ys.at[n, 2 + half], yr.at[n, 2 + half], head=to)

    outs = []

    def rs_last(n):
        arrive(r2.at[n, 0], yr.at[n, 2])
        arrive(r2.at[n, 1], yr.at[n, 3])
        ob[n] = (pf[n % 3, q_rows(h), :] + r2[n, 0].astype(F32) + r2[n, 1].astype(F32)).astype(BF16)
        first = plane(ORDER[n // PARTS]) * PLANE + n % PARTS * CW
        cp = pltpu.make_async_copy(ob.at[n], o_hbm.at[:, pl.ds(pl.multiple_of(first, CW), CW)], out_sem.at[n])
        cp.start()
        outs.append(cp)

    marks = [0]
    for n in range(NCH + 2):
        gather(f"chunk_{n}")
        if n < NCH:
            if n % PARTS == 0:
                with jax.named_scope(f"plane_wait_{n}"):
                    sib_recv(ORDER[n // PARTS])
            with jax.named_scope(f"project_{n}"):
                project(n)
                rs_first(n)
        if 1 <= n <= NCH:
            with jax.named_scope(f"reduce_{n}"):
                rs_second(n - 1)
        gather(f"after_{n}")
        if n >= 2:
            with jax.named_scope(f"finish_{n}"):
                for cp in sends[marks[max(0, n - 5)] : marks[max(0, n - 4)]]:
                    cp.wait_send()
                rs_last(n - 2)
        marks.append(len(sends))

    with jax.named_scope("drain"):
        for cp in outs:
            cp.wait()
        for cp in sends[marks[max(0, NCH + 1 - 4)] :]:
            cp.wait_send()


def per_device(queries, key_rows, values, gate_input, norm_gain, out_weight):
    anyspec = pl.BlockSpec(memory_space=pl.ANY)
    dma = lambda *n: pltpu.SemaphoreType.DMA(n)
    return pl.pallas_call(
        kernel,
        out_shape=jax.ShapeDtypeStruct((QT, D), BF16),
        in_specs=[anyspec] * 4 + [pl.BlockSpec(memory_space=pltpu.VMEM), anyspec],
        out_specs=anyspec,
        scratch_shapes=[
            pltpu.VMEM((TOK, WID), BF16),
            pltpu.VMEM((TOK, WID), BF16),
            pltpu.VMEM((TOK, WID), BF16),
            pltpu.VMEM((TOK, WID), BF16),
            pltpu.VMEM((NZ, NX, NC, SH, WID), BF16),
            pltpu.VMEM((WID, HD), BF16),
            pltpu.VMEM((WID, HD), BF16),
            pltpu.VMEM((TOK, WID), F32),
            pltpu.VMEM((TOK, WID), F32),
            pltpu.VMEM((TOK, WID), BF16),
            pltpu.VMEM((NP, PIECE, HD), BF16),
            pltpu.VMEM((NP, PIECE, HD), BF16),
            pltpu.VMEM((PIECE, HD), F32),
            pltpu.VMEM((NZ, SUB, HD), F32),
            pltpu.VMEM((NZ, SUB, HD), F32),
            pltpu.VMEM((PIECE, HD), F32),
            pltpu.VMEM((3, TOK, CW), F32),
            pltpu.VMEM((NCH, 2, QH, CW), BF16),
            pltpu.VMEM((NCH, 2, QT, CW), BF16),
            pltpu.VMEM((NCH, 2, QH, CW), BF16),
            pltpu.VMEM((NCH, 2, QT, CW), BF16),
            pltpu.VMEM((NCH, QT, CW), BF16),
            dma(5), dma(NCH),
            dma(9), dma(9),
            dma(NZ, 4), dma(NZ, 4),
            dma(9, NX), dma(9, NX),
            dma(NZ, NX), dma(NZ, NX),
            dma(NP), dma(NP), dma(NZ), dma(NZ), dma(NZ), dma(NZ), dma(NP), dma(NP),
            dma(NCH, 4), dma(NCH, 4),
        ],
        compiler_params=pltpu.CompilerParams(
            collective_id=0, has_side_effects=True, vmem_limit_bytes=60 * 1024 * 1024
        ),
    )(queries, key_rows, values, gate_input, norm_gain, out_weight.T)


def solution(mesh):
    in_specs = (
        P("seq", "head"),
        P("seq", "head"),
        P("seq", "head"),
        P("seq", "head"),
        P("head"),
        P("head", "seq"),
    )
    return jax.shard_map(
        per_device,
        mesh=mesh,
        in_specs=in_specs,
        out_specs=P(("seq", "head"), None),
        check_vma=False,
    )
```

```python
import functools

import jax
import jax.numpy as jnp
from jax import lax
from jax.experimental import pallas as pl
from jax.experimental.pallas import tpu as pltpu
from jax.sharding import PartitionSpec as P

HD = 128
NZ, NX, NC, NY = 8, 4, 2, 4
NP = NX * NC
TOK = 512
WID = 1536
HEADS = WID // HD
SH = 96
PLANE = NP * SH
D = NZ * PLANE
QT = TOK // NY
PIECE = WID // NP
SUB = PIECE // NZ
HALF = SH // 2
LAG2, LAG3 = 2, 4
SLOTS = LAG3 + 1
PARTS = 2
NCH = NZ * PARTS
CW = PLANE // PARTS
QH = QT // 2
F32, BF16 = jnp.float32, jnp.bfloat16
KINDS = "BAABBBBB"
ORDER = (0, 4, 1, 2, 6, 3, 5, 7)
PLAN = {
    "plane_recv": "O0 I0 Z4 X0",
    "z_scan": "Z2 I2 Z5 G0 Z3 F0 I3 Z8",
    "z_back": "Z9 X4 S0 A0 Z7",
    "state_recv": "Z6 Z12 Z13 I1 F4 X6",
    "project_1": "S4",
    "reduce_2": "X3",
    "reduce_3": "S1",
    "reduce_4": "S2 F6",
    "reduce_5": "F3",
    "project_6": "Z11",
    "reduce_6": "Z10",
    "project_7": "X5",
    "reduce_7": "S6 S3",
    "finish_8": "F5",
    "project_9": "Z14",
    "project_10": "X7",
    "finish_10": "S5",
    "project_12": "F7",
    "finish_13": "S7",
}
NT = (((1,), (1,)), ((), ()))
TN = (((0,), (0,)), ((), ()))


def kernel(
    q_hbm, k_hbm, v_hbm, g_hbm, gain_ref, w_hbm, o_hbm,
    qb, kb, vb, gb, wt, st, sin, intra, gate, nrm,
    pr1, pr3, zt, za, zb, zp, pf, t1, t2, r1, r2, ob,
    ld, out_sem, zs, zr, xs, xr, fs, fr, ss, sr, p1s, p1r, p2s, p2r, p3s, p3r, p4s, p4r, ys, yr,
):
    s = lax.axis_index("seq")
    h = lax.axis_index("head")
    c = lax.rem(s, NC)
    x = lax.rem(s // NC, NX)
    z = s // NP
    p = lax.rem(s, NP)

    def at_zx(zz, xx, cc):
        return (zz * NX + xx) * NC + cc

    zu, zd = lax.rem(z + 1, NZ), lax.rem(z + NZ - 1, NZ)
    xu, xd = lax.rem(x + 1, NX), lax.rem(x + NX - 1, NX)
    hu, hd, h2 = lax.rem(h + 1, NY), lax.rem(h + NY - 1, NY), lax.rem(h + 2, NY)
    dev_zu, dev_zd = at_zx(zu, x, c), at_zx(zd, x, c)
    dev_xu, dev_xd = at_zx(z, xu, c), at_zx(z, xd, c)
    dev_sib = at_zx(z, x, 1 - c)

    sends = []

    def remote(src, dst, send_sem, recv_sem, seq=s, head=h):
        return pltpu.make_async_remote_copy(
            src_ref=src, dst_ref=dst, send_sem=send_sem, recv_sem=recv_sem,
            device_id=(seq, head), device_id_type=pl.DeviceIdType.MESH,
        )

    def send(*args, **kw):
        cp = remote(*args, **kw)
        cp.start()
        sends.append(cp)

    def arrive(dst, recv_sem):
        remote(dst, dst, recv_sem, recv_sem, seq=dev_sib).wait_recv()

    def plane(j):
        off = -(j + 1) // 2 if j % 2 else j // 2
        return lax.rem(z + off + NZ, NZ)

    loads = [
        pltpu.make_async_copy(src, dst, ld.at[i])
        for i, (src, dst) in enumerate(
            ((k_hbm, kb), (v_hbm, vb), (w_hbm, wt.at[z, x, c]), (q_hbm, qb), (g_hbm, gb))
        )
    ]
    for cp in loads:
        cp.start()

    bar = pltpu.get_barrier_semaphore()
    for i in range(1, NP):
        pl.semaphore_signal(bar, inc=1, device_id=(z * NP + lax.rem(p + i, NP), h), device_id_type=pl.DeviceIdType.MESH)
    for i in range(1, NZ):
        pl.semaphore_signal(bar, inc=1, device_id=(lax.rem(z + i, NZ) * NP + p, h), device_id_type=pl.DeviceIdType.MESH)
    for hh in (hu, hd):
        pl.semaphore_signal(bar, inc=1, device_id=(s, hh), device_id_type=pl.DeviceIdType.MESH)

    def shard(pln, xx, cc):
        return wt.at[pln, xx, cc]

    def part(ref, half):
        return ref.at[pl.ds(half * HALF, HALF)]

    def z_start():
        own = shard(z, x, c)
        for i in range(2):
            up, dn = part(own, i), part(own, 1 - i)
            send(up, up, zs.at[1, i], zr.at[1, i], seq=dev_zu)
            send(dn, dn, zs.at[2, i], zr.at[2, i], seq=dev_zd)

    def z_recv(j, i):
        ref = shard(plane(j), x, c)
        if j == 7:
            arrive(part(ref, 0), zr.at[7, 0])
            arrive(part(ref, 1), zr.at[7, 1])
            return
        ref = part(ref, i if j % 2 else 1 - i)
        arrive(ref, zr.at[j, i])
        to = dev_zu if j % 2 else dev_zd
        if j < 5:
            send(ref, ref, zs.at[j + 2, i], zr.at[j + 2, i], seq=to)
        elif i == 0:
            send(ref, ref, zs.at[7, j - 5], zr.at[7, j - 5], seq=to)

    def sib_send(j, i):
        ref = shard(plane(j), lax.rem(x + i, NX), c)
        send(ref, ref, ss.at[j, i], sr.at[j, i], seq=dev_sib)

    def x_start(j):
        ref = shard(plane(j), x, c)
        for i in range(2):
            up, dn = part(ref, i), part(ref, 1 - i)
            send(up, up, xs.at[j, i], xr.at[j, i], seq=dev_xu)
            send(dn, dn, xs.at[j, 2 + i], xr.at[j, 2 + i], seq=dev_xd)
        sib_send(j, 0)

    def x_forward(j):
        pln = plane(j)
        ref = part(shard(pln, xd, c), 0)
        arrive(ref, xr.at[j, 0])
        send(ref, ref, xs.at[j, 4], xr.at[j, 4], seq=dev_xu)
        ref = part(shard(pln, xu, c), 1)
        arrive(ref, xr.at[j, 2])
        send(ref, ref, xs.at[j, 5], xr.at[j, 5], seq=dev_xd)

    def halves(ref):
        return part(ref, 0), part(ref, 1)

    def whole_start(j):
        for i in range(1, NX):
            ref = shard(plane(j), lax.rem(x + i, NX), c)
            if j % 2 or j == 0:
                up = halves(ref)[0] if j == 5 else ref
                send(up, up, fs.at[j + 2 - (j == 0), i], fr.at[j + 2 - (j == 0), i], seq=dev_zu)
            if j % 2 == 0:
                dn = halves(ref)[1] if j == 6 else ref
                send(dn, dn, fs.at[j + 2, i], fr.at[j + 2, i], seq=dev_zd)

    def fill(j):
        pln = plane(j)
        if KINDS[j] == "B":
            lo, hi = halves(shard(pln, lax.rem(x + 2, NX), c))
            arrive(part(shard(pln, xd, c), 1), xr.at[j, 1])
            sib_send(j, 3)
            arrive(part(shard(pln, xu, c), 0), xr.at[j, 3])
            sib_send(j, 1)
            arrive(lo, xr.at[j, 4])
            arrive(hi, xr.at[j, 5])
            sib_send(j, 2)
            return
        sib_send(j, 0)
        for i in range(1, NX):
            ref = shard(pln, lax.rem(x + i, NX), c)
            if j == 7:
                lo, hi = halves(ref)
                arrive(lo, fr.at[7, i])
                arrive(hi, fr.at[8, i])
            else:
                arrive(ref, fr.at[j, i])
            sib_send(j, i)

    def sib_recv(j):
        for i in range(NX):
            arrive(shard(plane(j), lax.rem(x + i, NX), 1 - c), sr.at[j, i])

    stages = {"O": lambda j: z_start(), "Z": lambda j: z_recv(j // 2, j % 2), "X": x_start, "F": x_forward, "A": whole_start, "S": fill}

    def gather(at):
        for name in PLAN.get(at, "").split():
            with jax.named_scope(f"gather_{name}"):
                stages[name[0]](int(name[1:]))

    with jax.named_scope("local_state"):
        loads[0].wait()
        loads[1].wait()

        def one_state(i, carry):
            cols = pl.ds(pl.multiple_of(i * HD, HD), HD)
            st[cols, :] = lax.dot_general(kb[:, cols], vb[:, cols], TN, preferred_element_type=F32).astype(BF16)
            return carry

        lax.fori_loop(0, HEADS, one_state, 0)

    with jax.named_scope("entry_barrier"):
        pl.semaphore_wait(bar, NP - 1 + NZ - 1 + 2)

    def piece_rows(i):
        return pl.ds(pl.multiple_of(i * PIECE, PIECE), PIECE)

    with jax.named_scope("plane_send"):
        for i in range(1, NP):
            to = lax.rem(p + i, NP)
            send(st.at[piece_rows(to)], pr1.at[p], p1s.at[i], p1r.at[i], seq=z * NP + to)
        pr1[p] = st[piece_rows(p), :]

    with jax.named_scope("weight_load"):
        loads[2].wait()
        loads[3].wait()
        loads[4].wait()

    HB = TOK // 2
    tri = lax.broadcasted_iota(jnp.int32, (HB, HB), 0) >= lax.broadcasted_iota(jnp.int32, (HB, HB), 1)

    def some_intra(first):
        lo, hi = pl.ds(0, HB), pl.ds(HB, HB)
        cols = [pl.ds((first + k) * HD, HD) for k in range(3)]
        low = [lax.dot_general(qb[lo, cl], kb[lo, cl], NT, preferred_element_type=F32) for cl in cols]
        low = [jnp.where(tri, a, 0.0).astype(BF16) for a in low]
        for cl, a in zip(cols, low):
            intra[lo, cl] = jnp.dot(a, vb[lo, cl], preferred_element_type=F32)
        full = [lax.dot_general(qb[hi, cl], kb[lo, cl], NT, preferred_element_type=F32).astype(BF16) for cl in cols]
        diag = [lax.dot_general(qb[hi, cl], kb[hi, cl], NT, preferred_element_type=F32) for cl in cols]
        diag = [jnp.where(tri, a, 0.0).astype(BF16) for a in diag]
        for cl, a, d in zip(cols, full, diag):
            intra[hi, cl] = jnp.dot(a, vb[lo, cl], preferred_element_type=F32) + jnp.dot(d, vb[hi, cl], preferred_element_type=F32)

    def one_gate(i, carry):
        cols = pl.ds(pl.multiple_of(i * HD, HD), HD)
        gi = gb[:, cols].astype(F32)
        gate[:, cols] = gi / (1.0 + jnp.exp(-gi)) * gain_ref[cols].reshape(1, HD)
        return carry

    def intra_part(i):
        some_intra(3 * i)

    stages["I"] = intra_part
    stages["G"] = lambda j: lax.fori_loop(0, HEADS, one_gate, 0)
    gather("plane_recv")

    def sub_rows(i):
        return pl.ds(pl.multiple_of(i * SUB, SUB), SUB)

    with jax.named_scope("plane_recv"):
        for i in range(1, NP):
            arrive(pr1.at[lax.rem(p + NP - i, NP)], p1r.at[i])
        total = pr1[0].astype(F32)
        for i in range(1, NP):
            total = total + pr1[i].astype(F32)
        zt[...] = total
        for i in range(1, NZ):
            to = lax.rem(z + i, NZ)
            send(zt.at[sub_rows(to)], za.at[z], p2s.at[i], p2r.at[i], seq=to * NP + p)
        za[z] = zt[sub_rows(z), :]

    gather("z_scan")
    with jax.named_scope("z_scan"):
        for i in range(1, NZ):
            arrive(za.at[lax.rem(z + NZ - i, NZ)], p2r.at[i])
        run = jnp.zeros((SUB, HD), F32)
        for i in range(NZ):
            zb[i] = run
            run = run + za[i]
        for i in range(1, NZ):
            to = lax.rem(z + i, NZ)
            send(zb.at[to], zp.at[sub_rows(z)], p3s.at[i], p3r.at[i], seq=to * NP + p)
        zp[sub_rows(z), :] = zb[z]

    gather("z_back")
    with jax.named_scope("z_back"):
        for i in range(1, NZ):
            arrive(zp.at[sub_rows(lax.rem(z + NZ - i, NZ))], p3r.at[i])
        run = zp[...]
        for i in range(NP):
            pr3[i] = run.astype(BF16)
            run = run + pr1[i].astype(F32)
        for i in range(1, NP):
            to = lax.rem(p + i, NP)
            send(pr3.at[to], sin.at[piece_rows(p)], p4s.at[i], p4r.at[i], seq=z * NP + to)
        sin[piece_rows(p), :] = pr3[p]

    gather("state_recv")
    with jax.named_scope("state_recv"):
        for i in range(1, NP):
            arrive(sin.at[piece_rows(lax.rem(p + NP - i, NP))], p4r.at[i])

    ones = jnp.full((HD, HD), 1.0 / HD, BF16)

    GROUP = 6

    def some_heads(i, carry):
        cols = [pl.ds(pl.multiple_of((i * GROUP + k) * HD, HD), HD) for k in range(GROUP)]
        att = [intra[:, cl] + jnp.dot(qb[:, cl], sin[cl, :], preferred_element_type=F32) for cl in cols]
        ms = [jnp.dot((a * a).astype(BF16), ones, preferred_element_type=F32) for a in att]
        for cl, a, m in zip(cols, att, ms):
            nrm[:, cl] = (a * lax.rsqrt(m + 1e-06) * gate[:, cl]).astype(BF16)
        return carry

    gather("attend_a")
    with jax.named_scope("attend"):
        lax.fori_loop(0, HEADS // GROUP // 2, some_heads, 0)
    gather("attend")
    with jax.named_scope("attend"):
        lax.fori_loop(HEADS // GROUP // 2, HEADS // GROUP, some_heads, 0)

    def q_rows(i):
        return pl.ds(pl.multiple_of(i * QT, QT), QT)

    def project(n):
        w = wt[plane(ORDER[n // PARTS]), pl.ds(n % PARTS * (NX // PARTS), NX // PARTS)].reshape(CW, WID)
        pf[n % SLOTS] = lax.dot_general(nrm[...], w, NT, preferred_element_type=F32)

    def half_rows(i, half):
        return pl.ds(pl.multiple_of(i * QT + half * QH, QH), QH)

    def rs_first(n):
        for half, to in ((0, hu), (1, hd)):
            t1[n, half] = pf[n % SLOTS, half_rows(h2, half), :].astype(BF16)
            send(t1.at[n, half], r1.at[n, half], ys.at[n, half], yr.at[n, half], head=to)

    def rs_second(n):
        for half, to in ((0, hu), (1, hd)):
            same, other = pl.ds(half * QH, QH), pl.ds((1 - half) * QH, QH)
            t2[n, half, other, :] = pf[n % SLOTS, half_rows(to, 1 - half), :].astype(BF16)
            arrive(r1.at[n, half], yr.at[n, half])
            t2[n, half, same, :] = (pf[n % SLOTS, half_rows(to, half), :] + r1[n, half].astype(F32)).astype(BF16)
            send(t2.at[n, half], r2.at[n, half], ys.at[n, 2 + half], yr.at[n, 2 + half], head=to)

    outs = []

    def rs_last(n):
        arrive(r2.at[n, 0], yr.at[n, 2])
        arrive(r2.at[n, 1], yr.at[n, 3])
        ob[n] = (pf[n % SLOTS, q_rows(h), :] + r2[n, 0].astype(F32) + r2[n, 1].astype(F32)).astype(BF16)
        first = plane(ORDER[n // PARTS]) * PLANE + n % PARTS * CW
        cp = pltpu.make_async_copy(ob.at[n], o_hbm.at[:, pl.ds(pl.multiple_of(first, CW), CW)], out_sem.at[n])
        cp.start()
        outs.append(cp)

    marks = [0]
    for n in range(NCH + LAG3):
        gather(f"project_{n}")
        if n < NCH:
            if n % PARTS == 0:
                with jax.named_scope(f"plane_wait_{n}"):
                    sib_recv(ORDER[n // PARTS])
            with jax.named_scope(f"project_{n}"):
                project(n)
                rs_first(n)
        gather(f"reduce_{n}")
        if LAG2 <= n < NCH + LAG2:
            with jax.named_scope(f"reduce_{n}"):
                rs_second(n - LAG2)
        gather(f"finish_{n}")
        if n >= LAG3:
            with jax.named_scope(f"finish_{n}"):
                for cp in sends[marks[max(0, n - LAG3 - 1)] : marks[n - LAG3]]:
                    cp.wait_send()
                rs_last(n - LAG3)
        marks.append(len(sends))

    with jax.named_scope("drain"):
        for cp in outs:
            cp.wait()
        for cp in sends[marks[NCH - 1] :]:
            cp.wait_send()


def land(src, dst, held, sem):
    rows = QT // 4
    parts = [pl.ds(i * rows, rows) for i in range(4)]
    into = [pltpu.make_async_copy(src.at[r], held.at[r], sem.at[0, i]) for i, r in enumerate(parts)]
    out = [pltpu.make_async_copy(held.at[r], dst.at[r], sem.at[1, i]) for i, r in enumerate(parts)]
    for cp in into:
        cp.start()
    for a, b in zip(into, out):
        a.wait()
        b.start()
    for cp in out:
        cp.wait()


def per_device(queries, key_rows, values, gate_input, norm_gain, out_weight):
    anyspec = pl.BlockSpec(memory_space=pl.ANY)
    dma = lambda *n: pltpu.SemaphoreType.DMA(n)
    out = pl.pallas_call(
        kernel,
        out_shape=jax.ShapeDtypeStruct((QT, D), BF16),
        in_specs=[anyspec] * 4 + [pl.BlockSpec(memory_space=pltpu.VMEM), anyspec],
        out_specs=anyspec,
        scratch_shapes=[
            pltpu.VMEM((TOK, WID), BF16),
            pltpu.VMEM((TOK, WID), BF16),
            pltpu.VMEM((TOK, WID), BF16),
            pltpu.VMEM((TOK, WID), BF16),
            pltpu.VMEM((NZ, NX, NC, SH, WID), BF16),
            pltpu.VMEM((WID, HD), BF16),
            pltpu.VMEM((WID, HD), BF16),
            pltpu.VMEM((TOK, WID), F32),
            pltpu.VMEM((TOK, WID), F32),
            pltpu.VMEM((TOK, WID), BF16),
            pltpu.VMEM((NP, PIECE, HD), BF16),
            pltpu.VMEM((NP, PIECE, HD), BF16),
            pltpu.VMEM((PIECE, HD), F32),
            pltpu.VMEM((NZ, SUB, HD), F32),
            pltpu.VMEM((NZ, SUB, HD), F32),
            pltpu.VMEM((PIECE, HD), F32),
            pltpu.VMEM((SLOTS, TOK, CW), F32),
            pltpu.VMEM((NCH, 2, QH, CW), BF16),
            pltpu.VMEM((NCH, 2, QT, CW), BF16),
            pltpu.VMEM((NCH, 2, QH, CW), BF16),
            pltpu.VMEM((NCH, 2, QT, CW), BF16),
            pltpu.VMEM((NCH, QT, CW), BF16),
            dma(5), dma(NCH),
            dma(NZ, 2), dma(NZ, 2),
            dma(NZ, 6), dma(NZ, 6),
            dma(9, NX), dma(9, NX),
            dma(NZ, NX), dma(NZ, NX),
            dma(NP), dma(NP), dma(NZ), dma(NZ), dma(NZ), dma(NZ), dma(NP), dma(NP),
            dma(NCH, 4), dma(NCH, 4),
        ],
        compiler_params=pltpu.CompilerParams(
            collective_id=0, has_side_effects=True, vmem_limit_bytes=60 * 1024 * 1024
        ),
    )(queries, key_rows, values, gate_input, norm_gain, out_weight.T)
    return pl.pallas_call(
        land,
        out_shape=jax.ShapeDtypeStruct((QT, D), BF16),
        in_specs=[anyspec],
        out_specs=anyspec,
        scratch_shapes=[pltpu.VMEM((QT, D), BF16), dma(2, 4)],
    )(out)


def solution(mesh):
    in_specs = (
        P("seq", "head"),
        P("seq", "head"),
        P("seq", "head"),
        P("seq", "head"),
        P("head"),
        P("head", "seq"),
    )
    return jax.shard_map(
        per_device,
        mesh=mesh,
        in_specs=in_specs,
        out_specs=P(("seq", "head"), None),
        check_vma=False,
    )
```

```python
import functools

import jax
import jax.numpy as jnp
from jax import lax
from jax.experimental import pallas as pl
from jax.experimental.pallas import tpu as pltpu
from jax.sharding import PartitionSpec as P

HD = 128
NZ, NX, NC, NY = 8, 4, 2, 4
NP = NX * NC
TOK = 512
WID = 1536
HEADS = WID // HD
SH = 96
PLANE = NP * SH
D = NZ * PLANE
QT = TOK // NY
PIECE = WID // NP
SUB = PIECE // NZ
HALF = SH // 2
LAG2, LAG3 = 2, 4
SLOTS = LAG3 + 1
PARTS = 2
FAR_X = (4, 5, 2, 6, 3, 7, 1)
FAR_Z = (4, 3, 5, 2, 6, 1, 7)
NCH = NZ * PARTS
CW = PLANE // PARTS
QH = QT // 2
F32, BF16 = jnp.float32, jnp.bfloat16
KINDS = "BAABBBBB"
ORDER = (0, 4, 1, 2, 6, 3, 5, 7)
PLAN = {
    "plane_recv": ("O0", "I0", "Z4", "X0", "X1",),
    "z_scan": ("Z2", "I2", "Z5", "G0", "Z3", "F0", "I3", "Z8",),
    "z_back": ("Z9", "X8", "X9", "S0", "A1", "A2", "A3", "Z7",),
    "state_recv": ("Z6", "Z12", "Z13", "I1", "F4", "X12", "X13",),
    "project_1": ("S4",),
    "reduce_2": ("X6", "X7",),
    "reduce_3": ("S1",),
    "reduce_4": ("S2", "F6",),
    "reduce_5": ("F3",),
    "project_6": ("Z11",),
    "reduce_6": ("Z10",),
    "project_7": ("X10", "X11",),
    "reduce_7": ("S6", "S3",),
    "finish_8": ("F5",),
    "project_9": ("Z14",),
    "project_10": ("X14", "X15",),
    "finish_10": ("S5",),
    "project_12": ("F7",),
    "finish_13": ("S7",),
}
NT = (((1,), (1,)), ((), ()))
TN = (((0,), (0,)), ((), ()))


def kernel(
    q_hbm, k_hbm, v_hbm, g_hbm, gain_ref, w_hbm, o_hbm,
    qb, kb, vb, gb, wt, st, sin, intra, gate, nrm,
    pr1, pr3, zt, za, zb, zp, pf, t1, t2, r1, r2, ob,
    ld, out_sem, zs, zr, xs, xr, fs, fr, ss, sr, p1s, p1r, p2s, p2r, p3s, p3r, p4s, p4r, ys, yr,
):
    s = lax.axis_index("seq")
    h = lax.axis_index("head")
    c = lax.rem(s, NC)
    x = lax.rem(s // NC, NX)
    z = s // NP
    p = lax.rem(s, NP)

    def at_zx(zz, xx, cc):
        return (zz * NX + xx) * NC + cc

    zu, zd = lax.rem(z + 1, NZ), lax.rem(z + NZ - 1, NZ)
    xu, xd = lax.rem(x + 1, NX), lax.rem(x + NX - 1, NX)
    hu, hd, h2 = lax.rem(h + 1, NY), lax.rem(h + NY - 1, NY), lax.rem(h + 2, NY)
    dev_zu, dev_zd = at_zx(zu, x, c), at_zx(zd, x, c)
    dev_xu, dev_xd = at_zx(z, xu, c), at_zx(z, xd, c)
    dev_sib = at_zx(z, x, 1 - c)

    sends = []

    def remote(src, dst, send_sem, recv_sem, seq=s, head=h):
        return pltpu.make_async_remote_copy(
            src_ref=src, dst_ref=dst, send_sem=send_sem, recv_sem=recv_sem,
            device_id=(seq, head), device_id_type=pl.DeviceIdType.MESH,
        )

    def send(*args, **kw):
        cp = remote(*args, **kw)
        cp.start()
        sends.append(cp)

    def arrive(dst, recv_sem):
        remote(dst, dst, recv_sem, recv_sem, seq=dev_sib).wait_recv()

    def plane(j):
        off = -(j + 1) // 2 if j % 2 else j // 2
        return lax.rem(z + off + NZ, NZ)

    loads = [
        pltpu.make_async_copy(src, dst, ld.at[i])
        for i, (src, dst) in enumerate(
            ((k_hbm, kb), (v_hbm, vb), (w_hbm, wt.at[z, x, c]), (q_hbm, qb), (g_hbm, gb))
        )
    ]
    for cp in loads:
        cp.start()

    bar = pltpu.get_barrier_semaphore()
    for i in range(1, NP):
        pl.semaphore_signal(bar, inc=1, device_id=(z * NP + lax.rem(p + i, NP), h), device_id_type=pl.DeviceIdType.MESH)
    for i in range(1, NZ):
        pl.semaphore_signal(bar, inc=1, device_id=(lax.rem(z + i, NZ) * NP + p, h), device_id_type=pl.DeviceIdType.MESH)
    for hh in (hu, hd):
        pl.semaphore_signal(bar, inc=1, device_id=(s, hh), device_id_type=pl.DeviceIdType.MESH)

    def shard(pln, xx, cc):
        return wt.at[pln, xx, cc]

    def part(ref, half):
        return ref.at[pl.ds(half * HALF, HALF)]

    def z_start():
        own = shard(z, x, c)
        for i in range(2):
            up, dn = part(own, i), part(own, 1 - i)
            send(up, up, zs.at[1, i], zr.at[1, i], seq=dev_zu)
            send(dn, dn, zs.at[2, i], zr.at[2, i], seq=dev_zd)

    def z_recv(j, i):
        ref = shard(plane(j), x, c)
        if j == 7:
            arrive(part(ref, 0), zr.at[7, 0])
            arrive(part(ref, 1), zr.at[7, 1])
            return
        ref = part(ref, i if j % 2 else 1 - i)
        arrive(ref, zr.at[j, i])
        to = dev_zu if j % 2 else dev_zd
        if j < 5:
            send(ref, ref, zs.at[j + 2, i], zr.at[j + 2, i], seq=to)
        elif i == 0:
            send(ref, ref, zs.at[7, j - 5], zr.at[7, j - 5], seq=to)

    def sib_send(j, i):
        ref = shard(plane(j), lax.rem(x + i, NX), c)
        send(ref, ref, ss.at[j, i], sr.at[j, i], seq=dev_sib)

    def x_start(j, i):
        ref = shard(plane(j), x, c)
        up, dn = part(ref, i), part(ref, 1 - i)
        send(up, up, xs.at[j, i], xr.at[j, i], seq=dev_xu)
        send(dn, dn, xs.at[j, 2 + i], xr.at[j, 2 + i], seq=dev_xd)
        if i == 0:
            sib_send(j, 0)

    def x_forward(j):
        pln = plane(j)
        ref = part(shard(pln, xd, c), 0)
        arrive(ref, xr.at[j, 0])
        send(ref, ref, xs.at[j, 4], xr.at[j, 4], seq=dev_xu)
        ref = part(shard(pln, xu, c), 1)
        arrive(ref, xr.at[j, 2])
        send(ref, ref, xs.at[j, 5], xr.at[j, 5], seq=dev_xd)

    def halves(ref):
        return part(ref, 0), part(ref, 1)

    def whole_start(j, i):
        ref = shard(plane(j), lax.rem(x + i, NX), c)
        if j % 2 or j == 0:
            up = part(ref, 0) if j == 5 else ref
            send(up, up, fs.at[j + 2 - (j == 0), i], fr.at[j + 2 - (j == 0), i], seq=dev_zu)
        if j % 2 == 0:
            dn = part(ref, 1) if j == 6 else ref
            send(dn, dn, fs.at[j + 2, i], fr.at[j + 2, i], seq=dev_zd)

    def fill(j):
        pln = plane(j)
        if KINDS[j] == "B":
            lo, hi = halves(shard(pln, lax.rem(x + 2, NX), c))
            arrive(part(shard(pln, xd, c), 1), xr.at[j, 1])
            sib_send(j, 3)
            arrive(part(shard(pln, xu, c), 0), xr.at[j, 3])
            sib_send(j, 1)
            arrive(lo, xr.at[j, 4])
            arrive(hi, xr.at[j, 5])
            sib_send(j, 2)
            return
        sib_send(j, 0)
        for i in range(1, NX):
            ref = shard(pln, lax.rem(x + i, NX), c)
            if j == 7:
                lo, hi = halves(ref)
                arrive(lo, fr.at[7, i])
                arrive(hi, fr.at[8, i])
            else:
                arrive(ref, fr.at[j, i])
            sib_send(j, i)

    def sib_recv(j):
        for i in range(NX):
            arrive(shard(plane(j), lax.rem(x + i, NX), 1 - c), sr.at[j, i])

    stages = {"O": lambda j: z_start(), "Z": lambda j: z_recv(j // 2, j % 2), "X": lambda j: x_start(j // 2, j % 2), "F": x_forward, "A": lambda j: whole_start(j // 4, j % 4), "S": fill}

    def gather(at):
        for name in PLAN.get(at, ()):
            with jax.named_scope(f"gather_{name}"):
                stages[name[0]](int(name[1:]))

    with jax.named_scope("local_state"):
        loads[0].wait()
        loads[1].wait()

        def one_state(i, carry):
            cols = pl.ds(pl.multiple_of(i * HD, HD), HD)
            st[cols, :] = lax.dot_general(kb[:, cols], vb[:, cols], TN, preferred_element_type=F32).astype(BF16)
            return carry

        lax.fori_loop(0, HEADS, one_state, 0)

    with jax.named_scope("entry_barrier"):
        pl.semaphore_wait(bar, NP - 1 + NZ - 1 + 2)

    def mate(i, way=1):
        return lax.rem(x + NX + way * (i // NC), NX) * NC + lax.rem(c + i, NC)

    def piece_rows(i):
        return pl.ds(pl.multiple_of(i * PIECE, PIECE), PIECE)

    with jax.named_scope("plane_send"):
        for i in FAR_X:
            to = mate(i)
            send(st.at[piece_rows(to)], pr1.at[p], p1s.at[i], p1r.at[i], seq=z * NP + to)
        pr1[p] = st[piece_rows(p), :]

    with jax.named_scope("weight_load"):
        loads[2].wait()
        loads[3].wait()
        loads[4].wait()

    HB = TOK // 2
    tri = lax.broadcasted_iota(jnp.int32, (HB, HB), 0) >= lax.broadcasted_iota(jnp.int32, (HB, HB), 1)

    def some_intra(first):
        lo, hi = pl.ds(0, HB), pl.ds(HB, HB)
        cols = [pl.ds((first + k) * HD, HD) for k in range(3)]
        low = [lax.dot_general(qb[lo, cl], kb[lo, cl], NT, preferred_element_type=F32) for cl in cols]
        low = [jnp.where(tri, a, 0.0).astype(BF16) for a in low]
        for cl, a in zip(cols, low):
            intra[lo, cl] = jnp.dot(a, vb[lo, cl], preferred_element_type=F32)
        full = [lax.dot_general(qb[hi, cl], kb[lo, cl], NT, preferred_element_type=F32).astype(BF16) for cl in cols]
        diag = [lax.dot_general(qb[hi, cl], kb[hi, cl], NT, preferred_element_type=F32) for cl in cols]
        diag = [jnp.where(tri, a, 0.0).astype(BF16) for a in diag]
        for cl, a, d in zip(cols, full, diag):
            intra[hi, cl] = jnp.dot(a, vb[lo, cl], preferred_element_type=F32) + jnp.dot(d, vb[hi, cl], preferred_element_type=F32)

    def one_gate(i, carry):
        cols = pl.ds(pl.multiple_of(i * HD, HD), HD)
        gi = gb[:, cols].astype(F32)
        gate[:, cols] = gi / (1.0 + jnp.exp(-gi)) * gain_ref[cols].reshape(1, HD)
        return carry

    def intra_part(i):
        some_intra(3 * i)

    stages["I"] = intra_part
    stages["G"] = lambda j: lax.fori_loop(0, HEADS, one_gate, 0)
    gather("plane_recv")

    def sub_rows(i):
        return pl.ds(pl.multiple_of(i * SUB, SUB), SUB)

    with jax.named_scope("plane_recv"):
        for i in FAR_X:
            arrive(pr1.at[mate(i, -1)], p1r.at[i])
        total = pr1[0].astype(F32)
        for i in range(1, NP):
            total = total + pr1[i].astype(F32)
        zt[...] = total
        for i in FAR_Z:
            to = lax.rem(z + i, NZ)
            send(zt.at[sub_rows(to)], za.at[z], p2s.at[i], p2r.at[i], seq=to * NP + p)
        za[z] = zt[sub_rows(z), :]

    gather("z_scan")
    with jax.named_scope("z_scan"):
        for i in FAR_Z:
            arrive(za.at[lax.rem(z + NZ - i, NZ)], p2r.at[i])
        run = jnp.zeros((SUB, HD), F32)
        for i in range(NZ):
            zb[i] = run
            run = run + za[i]
        for i in FAR_Z:
            to = lax.rem(z + i, NZ)
            send(zb.at[to], zp.at[sub_rows(z)], p3s.at[i], p3r.at[i], seq=to * NP + p)
        zp[sub_rows(z), :] = zb[z]

    gather("z_back")
    with jax.named_scope("z_back"):
        for i in FAR_Z:
            arrive(zp.at[sub_rows(lax.rem(z + NZ - i, NZ))], p3r.at[i])
        run = zp[...]
        for i in range(NP):
            pr3[i] = run.astype(BF16)
            run = run + pr1[i].astype(F32)
        for i in FAR_X:
            to = mate(i)
            send(pr3.at[to], sin.at[piece_rows(p)], p4s.at[i], p4r.at[i], seq=z * NP + to)
        sin[piece_rows(p), :] = pr3[p]

    gather("state_recv")
    with jax.named_scope("state_recv"):
        for i in FAR_X:
            arrive(sin.at[piece_rows(mate(i, -1))], p4r.at[i])

    ones = jnp.full((HD, HD), 1.0 / HD, BF16)

    GROUP = 6

    def some_heads(i, carry):
        cols = [pl.ds(pl.multiple_of((i * GROUP + k) * HD, HD), HD) for k in range(GROUP)]
        att = [intra[:, cl] + jnp.dot(qb[:, cl], sin[cl, :], preferred_element_type=F32) for cl in cols]
        ms = [jnp.dot((a * a).astype(BF16), ones, preferred_element_type=F32) for a in att]
        for cl, a, m in zip(cols, att, ms):
            nrm[:, cl] = (a * lax.rsqrt(m + 1e-06) * gate[:, cl]).astype(BF16)
        return carry

    gather("attend_a")
    with jax.named_scope("attend"):
        lax.fori_loop(0, HEADS // GROUP // 2, some_heads, 0)
    gather("attend")
    with jax.named_scope("attend"):
        lax.fori_loop(HEADS // GROUP // 2, HEADS // GROUP, some_heads, 0)

    def q_rows(i):
        return pl.ds(pl.multiple_of(i * QT, QT), QT)

    def project(n):
        w = wt[plane(ORDER[n // PARTS]), pl.ds(n % PARTS * (NX // PARTS), NX // PARTS)].reshape(CW, WID)
        pf[n % SLOTS] = lax.dot_general(nrm[...], w, NT, preferred_element_type=F32)

    def half_rows(i, half):
        return pl.ds(pl.multiple_of(i * QT + half * QH, QH), QH)

    def rs_first(n):
        for half, to in ((0, hu), (1, hd)):
            t1[n, half] = pf[n % SLOTS, half_rows(h2, half), :].astype(BF16)
            send(t1.at[n, half], r1.at[n, half], ys.at[n, half], yr.at[n, half], head=to)

    def rs_second(n):
        for half, to in ((0, hu), (1, hd)):
            same, other = pl.ds(half * QH, QH), pl.ds((1 - half) * QH, QH)
            t2[n, half, other, :] = pf[n % SLOTS, half_rows(to, 1 - half), :].astype(BF16)
            arrive(r1.at[n, half], yr.at[n, half])
            t2[n, half, same, :] = (pf[n % SLOTS, half_rows(to, half), :] + r1[n, half].astype(F32)).astype(BF16)
            send(t2.at[n, half], r2.at[n, half], ys.at[n, 2 + half], yr.at[n, 2 + half], head=to)

    outs = []

    def rs_last(n):
        arrive(r2.at[n, 0], yr.at[n, 2])
        arrive(r2.at[n, 1], yr.at[n, 3])
        ob[n] = (pf[n % SLOTS, q_rows(h), :] + r2[n, 0].astype(F32) + r2[n, 1].astype(F32)).astype(BF16)
        first = plane(ORDER[n // PARTS]) * PLANE + n % PARTS * CW
        cp = pltpu.make_async_copy(ob.at[n], o_hbm.at[:, pl.ds(pl.multiple_of(first, CW), CW)], out_sem.at[n])
        cp.start()
        outs.append(cp)

    marks = [0]
    for n in range(NCH + LAG3):
        gather(f"project_{n}")
        if n < NCH:
            if n % PARTS == 0:
                with jax.named_scope(f"plane_wait_{n}"):
                    sib_recv(ORDER[n // PARTS])
            with jax.named_scope(f"project_{n}"):
                project(n)
                rs_first(n)
        gather(f"reduce_{n}")
        if LAG2 <= n < NCH + LAG2:
            with jax.named_scope(f"reduce_{n}"):
                rs_second(n - LAG2)
        gather(f"finish_{n}")
        if n >= LAG3:
            with jax.named_scope(f"finish_{n}"):
                for cp in sends[marks[max(0, n - LAG3 - 1)] : marks[n - LAG3]]:
                    cp.wait_send()
                rs_last(n - LAG3)
        marks.append(len(sends))

    with jax.named_scope("drain"):
        for cp in outs:
            cp.wait()
        for cp in sends[marks[NCH - 1] :]:
            cp.wait_send()


def land(src, dst, held, sem):
    rows = QT // 4
    parts = [pl.ds(i * rows, rows) for i in range(4)]
    into = [pltpu.make_async_copy(src.at[r], held.at[r], sem.at[0, i]) for i, r in enumerate(parts)]
    out = [pltpu.make_async_copy(held.at[r], dst.at[r], sem.at[1, i]) for i, r in enumerate(parts)]
    for cp in into:
        cp.start()
    for a, b in zip(into, out):
        a.wait()
        b.start()
    for cp in out:
        cp.wait()


def per_device(queries, key_rows, values, gate_input, norm_gain, out_weight):
    anyspec = pl.BlockSpec(memory_space=pl.ANY)
    dma = lambda *n: pltpu.SemaphoreType.DMA(n)
    out = pl.pallas_call(
        kernel,
        out_shape=jax.ShapeDtypeStruct((QT, D), BF16),
        in_specs=[anyspec] * 4 + [pl.BlockSpec(memory_space=pltpu.VMEM), anyspec],
        out_specs=anyspec,
        scratch_shapes=[
            pltpu.VMEM((TOK, WID), BF16),
            pltpu.VMEM((TOK, WID), BF16),
            pltpu.VMEM((TOK, WID), BF16),
            pltpu.VMEM((TOK, WID), BF16),
            pltpu.VMEM((NZ, NX, NC, SH, WID), BF16),
            pltpu.VMEM((WID, HD), BF16),
            pltpu.VMEM((WID, HD), BF16),
            pltpu.VMEM((TOK, WID), F32),
            pltpu.VMEM((TOK, WID), F32),
            pltpu.VMEM((TOK, WID), BF16),
            pltpu.VMEM((NP, PIECE, HD), BF16),
            pltpu.VMEM((NP, PIECE, HD), BF16),
            pltpu.VMEM((PIECE, HD), F32),
            pltpu.VMEM((NZ, SUB, HD), F32),
            pltpu.VMEM((NZ, SUB, HD), F32),
            pltpu.VMEM((PIECE, HD), F32),
            pltpu.VMEM((SLOTS, TOK, CW), F32),
            pltpu.VMEM((NCH, 2, QH, CW), BF16),
            pltpu.VMEM((NCH, 2, QT, CW), BF16),
            pltpu.VMEM((NCH, 2, QH, CW), BF16),
            pltpu.VMEM((NCH, 2, QT, CW), BF16),
            pltpu.VMEM((NCH, QT, CW), BF16),
            dma(5), dma(NCH),
            dma(NZ, 2), dma(NZ, 2),
            dma(NZ, 6), dma(NZ, 6),
            dma(9, NX), dma(9, NX),
            dma(NZ, NX), dma(NZ, NX),
            dma(NP), dma(NP), dma(NZ), dma(NZ), dma(NZ), dma(NZ), dma(NP), dma(NP),
            dma(NCH, 4), dma(NCH, 4),
        ],
        compiler_params=pltpu.CompilerParams(
            collective_id=0, has_side_effects=True, vmem_limit_bytes=60 * 1024 * 1024
        ),
    )(queries, key_rows, values, gate_input, norm_gain, out_weight.T)
    return pl.pallas_call(
        land,
        out_shape=jax.ShapeDtypeStruct((QT, D), BF16),
        in_specs=[anyspec],
        out_specs=anyspec,
        scratch_shapes=[pltpu.VMEM((QT, D), BF16), dma(2, 4)],
    )(out)


def solution(mesh):
    in_specs = (
        P("seq", "head"),
        P("seq", "head"),
        P("seq", "head"),
        P("seq", "head"),
        P("head"),
        P("head", "seq"),
    )
    return jax.shard_map(
        per_device,
        mesh=mesh,
        in_specs=in_specs,
        out_specs=P(("seq", "head"), None),
        check_vma=False,
    )
```

```python
import functools

import jax
import jax.numpy as jnp
from jax import lax
from jax.experimental import pallas as pl
from jax.experimental.pallas import tpu as pltpu
from jax.sharding import PartitionSpec as P

HD = 128
NZ, NX, NC, NY = 8, 4, 2, 4
NP = NX * NC
TOK = 512
WID = 1536
HEADS = WID // HD
SH = 96
PLANE = NP * SH
D = NZ * PLANE
QT = TOK // NY
PIECE = WID // NP
SUB = PIECE // NZ
HALF = SH // 2
LAG2, LAG3 = 2, 4
SLOTS = LAG3 + 1
PARTS = 2
FAR_X = (4, 5, 2, 6, 3, 7, 1)
FAR_Z = (4, 3, 5, 2, 6, 1, 7)
NCH = NZ * PARTS
CW = PLANE // PARTS
QH = QT // 2
F32, BF16 = jnp.float32, jnp.bfloat16
KINDS = "BAABBBBB"
ORDER = (0, 4, 1, 2, 6, 3, 5, 7)
PLAN = {
    "plane_recv": ("O0", "I0", "Z4", "X0", "X1",),
    "z_scan": ("Z2", "I2", "Z5", "G0", "Z3", "F0", "I3", "Z8",),
    "z_back": ("Z9", "X8", "X9", "S0", "A1", "A2", "A3", "Z7",),
    "state_recv": ("Z6", "Z12", "Z13", "I1", "F4", "X12", "X13",),
    "project_1": ("S4",),
    "reduce_2": ("X6", "X7",),
    "reduce_3": ("S1",),
    "reduce_4": ("S2", "F6",),
    "reduce_5": ("F3",),
    "project_6": ("Z11",),
    "reduce_6": ("Z10",),
    "project_7": ("X10", "X11",),
    "reduce_7": ("S6", "S3",),
    "finish_8": ("F5",),
    "project_9": ("Z14",),
    "project_10": ("X14", "X15",),
    "finish_10": ("S5",),
    "project_12": ("F7",),
    "finish_13": ("S7",),
}
NT = (((1,), (1,)), ((), ()))
TN = (((0,), (0,)), ((), ()))


def kernel(
    q_hbm, k_hbm, v_hbm, g_hbm, gain_ref, w_hbm, o_hbm,
    qb, kb, vb, gb, wt, st, sin, intra, gate, nrm,
    pr1, pr3, zt, za, zb, zp, pf, t1, t2, r1, r2, ob,
    ld, out_sem, zs, zr, xs, xr, fs, fr, ss, sr, p1s, p1r, p2s, p2r, p3s, p3r, p4s, p4r, ys, yr,
):
    s = lax.axis_index("seq")
    h = lax.axis_index("head")
    c = lax.rem(s, NC)
    x = lax.rem(s // NC, NX)
    z = s // NP
    p = lax.rem(s, NP)

    def at_zx(zz, xx, cc):
        return (zz * NX + xx) * NC + cc

    zu, zd = lax.rem(z + 1, NZ), lax.rem(z + NZ - 1, NZ)
    xu, xd = lax.rem(x + 1, NX), lax.rem(x + NX - 1, NX)
    hu, hd, h2 = lax.rem(h + 1, NY), lax.rem(h + NY - 1, NY), lax.rem(h + 2, NY)
    dev_zu, dev_zd = at_zx(zu, x, c), at_zx(zd, x, c)
    dev_xu, dev_xd = at_zx(z, xu, c), at_zx(z, xd, c)
    dev_sib = at_zx(z, x, 1 - c)

    sends = []

    def remote(src, dst, send_sem, recv_sem, seq=s, head=h):
        return pltpu.make_async_remote_copy(
            src_ref=src, dst_ref=dst, send_sem=send_sem, recv_sem=recv_sem,
            device_id=(seq, head), device_id_type=pl.DeviceIdType.MESH,
        )

    def send(*args, **kw):
        cp = remote(*args, **kw)
        cp.start()
        sends.append(cp)

    def arrive(dst, recv_sem):
        remote(dst, dst, recv_sem, recv_sem, seq=dev_sib).wait_recv()

    def plane(j):
        off = -(j + 1) // 2 if j % 2 else j // 2
        return lax.rem(z + off + NZ, NZ)

    loads = [
        pltpu.make_async_copy(src, dst, ld.at[i])
        for i, (src, dst) in enumerate(
            ((k_hbm, kb), (v_hbm, vb), (w_hbm, wt.at[z, x, c]), (q_hbm, qb), (g_hbm, gb))
        )
    ]
    for cp in loads:
        cp.start()

    bar = pltpu.get_barrier_semaphore()
    for i in range(1, NP):
        pl.semaphore_signal(bar, inc=1, device_id=(z * NP + lax.rem(p + i, NP), h), device_id_type=pl.DeviceIdType.MESH)
    for i in range(1, NZ):
        pl.semaphore_signal(bar, inc=1, device_id=(lax.rem(z + i, NZ) * NP + p, h), device_id_type=pl.DeviceIdType.MESH)
    for hh in (hu, hd):
        pl.semaphore_signal(bar, inc=1, device_id=(s, hh), device_id_type=pl.DeviceIdType.MESH)

    def shard(pln, xx, cc):
        return wt.at[pln, xx, cc]

    def part(ref, half):
        return ref.at[pl.ds(half * HALF, HALF)]

    def z_start():
        own = shard(z, x, c)
        for i in range(2):
            up, dn = part(own, i), part(own, 1 - i)
            send(up, up, zs.at[1, i], zr.at[1, i], seq=dev_zu)
            send(dn, dn, zs.at[2, i], zr.at[2, i], seq=dev_zd)

    def z_recv(j, i):
        ref = shard(plane(j), x, c)
        if j == 7:
            arrive(part(ref, 0), zr.at[7, 0])
            arrive(part(ref, 1), zr.at[7, 1])
            return
        ref = part(ref, i if j % 2 else 1 - i)
        arrive(ref, zr.at[j, i])
        to = dev_zu if j % 2 else dev_zd
        if j < 5:
            send(ref, ref, zs.at[j + 2, i], zr.at[j + 2, i], seq=to)
        elif i == 0:
            send(ref, ref, zs.at[7, j - 5], zr.at[7, j - 5], seq=to)

    def sib_send(j, i):
        ref = shard(plane(j), lax.rem(x + i, NX), c)
        send(ref, ref, ss.at[j, i], sr.at[j, i], seq=dev_sib)

    def x_start(j, i):
        ref = shard(plane(j), x, c)
        up, dn = part(ref, i), part(ref, 1 - i)
        send(up, up, xs.at[j, i], xr.at[j, i], seq=dev_xu)
        send(dn, dn, xs.at[j, 2 + i], xr.at[j, 2 + i], seq=dev_xd)
        if i == 0:
            sib_send(j, 0)

    def x_forward(j):
        pln = plane(j)
        ref = part(shard(pln, xd, c), 0)
        arrive(ref, xr.at[j, 0])
        send(ref, ref, xs.at[j, 4], xr.at[j, 4], seq=dev_xu)
        ref = part(shard(pln, xu, c), 1)
        arrive(ref, xr.at[j, 2])
        send(ref, ref, xs.at[j, 5], xr.at[j, 5], seq=dev_xd)

    def halves(ref):
        return part(ref, 0), part(ref, 1)

    def whole_start(j, i):
        ref = shard(plane(j), lax.rem(x + i, NX), c)
        if j % 2 or j == 0:
            up = part(ref, 0) if j == 5 else ref
            send(up, up, fs.at[j + 2 - (j == 0), i], fr.at[j + 2 - (j == 0), i], seq=dev_zu)
        if j % 2 == 0:
            dn = part(ref, 1) if j == 6 else ref
            send(dn, dn, fs.at[j + 2, i], fr.at[j + 2, i], seq=dev_zd)

    def fill(j):
        pln = plane(j)
        if KINDS[j] == "B":
            lo, hi = halves(shard(pln, lax.rem(x + 2, NX), c))
            arrive(part(shard(pln, xd, c), 1), xr.at[j, 1])
            sib_send(j, 3)
            arrive(part(shard(pln, xu, c), 0), xr.at[j, 3])
            sib_send(j, 1)
            arrive(lo, xr.at[j, 4])
            arrive(hi, xr.at[j, 5])
            sib_send(j, 2)
            return
        sib_send(j, 0)
        for i in range(1, NX):
            ref = shard(pln, lax.rem(x + i, NX), c)
            if j == 7:
                lo, hi = halves(ref)
                arrive(lo, fr.at[7, i])
                arrive(hi, fr.at[8, i])
            else:
                arrive(ref, fr.at[j, i])
            sib_send(j, i)

    def sib_recv(j):
        for i in range(NX):
            arrive(shard(plane(j), lax.rem(x + i, NX), 1 - c), sr.at[j, i])

    stages = {"O": lambda j: z_start(), "Z": lambda j: z_recv(j // 2, j % 2), "X": lambda j: x_start(j // 2, j % 2), "F": x_forward, "A": lambda j: whole_start(j // 4, j % 4), "S": fill}

    def gather(at):
        for name in PLAN.get(at, ()):
            with jax.named_scope(f"gather_{name}"):
                stages[name[0]](int(name[1:]))

    with jax.named_scope("local_state"):
        loads[0].wait()
        loads[1].wait()

        def one_state(i, carry):
            cols = pl.ds(pl.multiple_of(i * HD, HD), HD)
            st[cols, :] = lax.dot_general(kb[:, cols], vb[:, cols], TN, preferred_element_type=F32).astype(BF16)
            return carry

        lax.fori_loop(0, HEADS, one_state, 0)

    with jax.named_scope("entry_barrier"):
        pl.semaphore_wait(bar, NP - 1 + NZ - 1 + 2)

    def mate(i, way=1):
        return lax.rem(x + NX + way * (i // NC), NX) * NC + lax.rem(c + i, NC)

    def piece_rows(i):
        return pl.ds(pl.multiple_of(i * PIECE, PIECE), PIECE)

    with jax.named_scope("plane_send"):
        for i in FAR_X:
            to = mate(i)
            send(st.at[piece_rows(to)], pr1.at[p], p1s.at[i], p1r.at[i], seq=z * NP + to)
        pr1[p] = st[piece_rows(p), :]

    with jax.named_scope("weight_load"):
        loads[2].wait()
        loads[3].wait()
        loads[4].wait()

    HB = TOK // 2
    tri = lax.broadcasted_iota(jnp.int32, (HB, HB), 0) >= lax.broadcasted_iota(jnp.int32, (HB, HB), 1)

    def some_intra(first):
        lo, hi = pl.ds(0, HB), pl.ds(HB, HB)
        cols = [pl.ds((first + k) * HD, HD) for k in range(3)]
        low = [lax.dot_general(qb[lo, cl], kb[lo, cl], NT, preferred_element_type=F32) for cl in cols]
        low = [jnp.where(tri, a, 0.0).astype(BF16) for a in low]
        for cl, a in zip(cols, low):
            intra[lo, cl] = jnp.dot(a, vb[lo, cl], preferred_element_type=F32)
        full = [lax.dot_general(qb[hi, cl], kb[lo, cl], NT, preferred_element_type=F32).astype(BF16) for cl in cols]
        diag = [lax.dot_general(qb[hi, cl], kb[hi, cl], NT, preferred_element_type=F32) for cl in cols]
        diag = [jnp.where(tri, a, 0.0).astype(BF16) for a in diag]
        for cl, a, d in zip(cols, full, diag):
            intra[hi, cl] = jnp.dot(a, vb[lo, cl], preferred_element_type=F32) + jnp.dot(d, vb[hi, cl], preferred_element_type=F32)

    def some_gates(i, carry):
        for k in range(3):
            cols = pl.ds(pl.multiple_of((3 * i + k) * HD, HD), HD)
            gi = gb[:, cols].astype(F32)
            gate[:, cols] = gi / (1.0 + jnp.exp(-gi)) * gain_ref[cols].reshape(1, HD)
        return carry

    def intra_part(i):
        some_intra(3 * i)

    stages["I"] = intra_part
    stages["G"] = lambda j: lax.fori_loop(0, HEADS // 3, some_gates, 0)
    gather("plane_recv")

    def sub_rows(i):
        return pl.ds(pl.multiple_of(i * SUB, SUB), SUB)

    with jax.named_scope("plane_recv"):
        for i in FAR_X:
            arrive(pr1.at[mate(i, -1)], p1r.at[i])
        total = pr1[0].astype(F32)
        for i in range(1, NP):
            total = total + pr1[i].astype(F32)
        zt[...] = total
        for i in FAR_Z:
            to = lax.rem(z + i, NZ)
            send(zt.at[sub_rows(to)], za.at[z], p2s.at[i], p2r.at[i], seq=to * NP + p)
        za[z] = zt[sub_rows(z), :]

    gather("z_scan")
    with jax.named_scope("z_scan"):
        for i in FAR_Z:
            arrive(za.at[lax.rem(z + NZ - i, NZ)], p2r.at[i])
        run = jnp.zeros((SUB, HD), F32)
        for i in range(NZ):
            zb[i] = run
            run = run + za[i]
        for i in FAR_Z:
            to = lax.rem(z + i, NZ)
            send(zb.at[to], zp.at[sub_rows(z)], p3s.at[i], p3r.at[i], seq=to * NP + p)
        zp[sub_rows(z), :] = zb[z]

    gather("z_back")
    with jax.named_scope("z_back"):
        for i in FAR_Z:
            arrive(zp.at[sub_rows(lax.rem(z + NZ - i, NZ))], p3r.at[i])
        run = zp[...]
        for i in range(NP):
            pr3[i] = run.astype(BF16)
            run = run + pr1[i].astype(F32)
        for i in FAR_X:
            to = mate(i)
            send(pr3.at[to], sin.at[piece_rows(p)], p4s.at[i], p4r.at[i], seq=z * NP + to)
        sin[piece_rows(p), :] = pr3[p]

    gather("state_recv")
    with jax.named_scope("state_recv"):
        for i in FAR_X:
            arrive(sin.at[piece_rows(mate(i, -1))], p4r.at[i])

    ones = jnp.full((HD, HD), 1.0 / HD, BF16)

    GROUP = 6

    def some_heads(i, carry):
        cols = [pl.ds(pl.multiple_of((i * GROUP + k) * HD, HD), HD) for k in range(GROUP)]
        att = [intra[:, cl] + jnp.dot(qb[:, cl], sin[cl, :], preferred_element_type=F32) for cl in cols]
        ms = [jnp.dot((a * a).astype(BF16), ones, preferred_element_type=F32) for a in att]
        for cl, a, m in zip(cols, att, ms):
            nrm[:, cl] = (a * lax.rsqrt(m + 1e-06) * gate[:, cl]).astype(BF16)
        return carry

    gather("attend_a")
    with jax.named_scope("attend"):
        lax.fori_loop(0, HEADS // GROUP // 2, some_heads, 0)
    gather("attend")
    with jax.named_scope("attend"):
        lax.fori_loop(HEADS // GROUP // 2, HEADS // GROUP, some_heads, 0)

    def q_rows(i):
        return pl.ds(pl.multiple_of(i * QT, QT), QT)

    def project(n):
        w = wt[plane(ORDER[n // PARTS]), pl.ds(n % PARTS * (NX // PARTS), NX // PARTS)].reshape(CW, WID)
        pf[n % SLOTS] = lax.dot_general(nrm[...], w, NT, preferred_element_type=F32)

    def half_rows(i, half):
        return pl.ds(pl.multiple_of(i * QT + half * QH, QH), QH)

    def rs_first(n):
        for half, to in ((0, hu), (1, hd)):
            t1[n, half] = pf[n % SLOTS, half_rows(h2, half), :].astype(BF16)
            send(t1.at[n, half], r1.at[n, half], ys.at[n, half], yr.at[n, half], head=to)

    def rs_second(n):
        for half, to in ((0, hu), (1, hd)):
            same, other = pl.ds(half * QH, QH), pl.ds((1 - half) * QH, QH)
            t2[n, half, other, :] = pf[n % SLOTS, half_rows(to, 1 - half), :].astype(BF16)
            arrive(r1.at[n, half], yr.at[n, half])
            t2[n, half, same, :] = (pf[n % SLOTS, half_rows(to, half), :] + r1[n, half].astype(F32)).astype(BF16)
            send(t2.at[n, half], r2.at[n, half], ys.at[n, 2 + half], yr.at[n, 2 + half], head=to)

    outs = []

    def rs_last(n):
        arrive(r2.at[n, 0], yr.at[n, 2])
        arrive(r2.at[n, 1], yr.at[n, 3])
        ob[n] = (pf[n % SLOTS, q_rows(h), :] + r2[n, 0].astype(F32) + r2[n, 1].astype(F32)).astype(BF16)
        first = plane(ORDER[n // PARTS]) * PLANE + n % PARTS * CW
        cp = pltpu.make_async_copy(ob.at[n], o_hbm.at[:, pl.ds(pl.multiple_of(first, CW), CW)], out_sem.at[n])
        cp.start()
        outs.append(cp)

    marks = [0]
    for n in range(NCH + LAG3):
        gather(f"project_{n}")
        if n < NCH:
            if n % PARTS == 0:
                with jax.named_scope(f"plane_wait_{n}"):
                    sib_recv(ORDER[n // PARTS])
            with jax.named_scope(f"project_{n}"):
                project(n)
                rs_first(n)
        gather(f"reduce_{n}")
        if LAG2 <= n < NCH + LAG2:
            with jax.named_scope(f"reduce_{n}"):
                rs_second(n - LAG2)
        gather(f"finish_{n}")
        if n >= LAG3:
            with jax.named_scope(f"finish_{n}"):
                for cp in sends[marks[max(0, n - LAG3 - 1)] : marks[n - LAG3]]:
                    cp.wait_send()
                rs_last(n - LAG3)
        marks.append(len(sends))

    with jax.named_scope("drain"):
        for cp in outs:
            cp.wait()
        for cp in sends[marks[NCH - 1] :]:
            cp.wait_send()


def land(src, dst, held, sem):
    rows = QT // 8
    parts = [pl.ds(i * rows, rows) for i in range(8)]
    into = [pltpu.make_async_copy(src.at[r], held.at[r], sem.at[0, i]) for i, r in enumerate(parts)]
    out = [pltpu.make_async_copy(held.at[r], dst.at[r], sem.at[1, i]) for i, r in enumerate(parts)]
    for cp in into:
        cp.start()
    for a, b in zip(into, out):
        a.wait()
        b.start()
    for cp in out:
        cp.wait()


def per_device(queries, key_rows, values, gate_input, norm_gain, out_weight):
    anyspec = pl.BlockSpec(memory_space=pl.ANY)
    dma = lambda *n: pltpu.SemaphoreType.DMA(n)
    out = pl.pallas_call(
        kernel,
        out_shape=jax.ShapeDtypeStruct((QT, D), BF16),
        in_specs=[anyspec] * 4 + [pl.BlockSpec(memory_space=pltpu.VMEM), anyspec],
        out_specs=anyspec,
        scratch_shapes=[
            pltpu.VMEM((TOK, WID), BF16),
            pltpu.VMEM((TOK, WID), BF16),
            pltpu.VMEM((TOK, WID), BF16),
            pltpu.VMEM((TOK, WID), BF16),
            pltpu.VMEM((NZ, NX, NC, SH, WID), BF16),
            pltpu.VMEM((WID, HD), BF16),
            pltpu.VMEM((WID, HD), BF16),
            pltpu.VMEM((TOK, WID), F32),
            pltpu.VMEM((TOK, WID), F32),
            pltpu.VMEM((TOK, WID), BF16),
            pltpu.VMEM((NP, PIECE, HD), BF16),
            pltpu.VMEM((NP, PIECE, HD), BF16),
            pltpu.VMEM((PIECE, HD), F32),
            pltpu.VMEM((NZ, SUB, HD), F32),
            pltpu.VMEM((NZ, SUB, HD), F32),
            pltpu.VMEM((PIECE, HD), F32),
            pltpu.VMEM((SLOTS, TOK, CW), F32),
            pltpu.VMEM((NCH, 2, QH, CW), BF16),
            pltpu.VMEM((NCH, 2, QT, CW), BF16),
            pltpu.VMEM((NCH, 2, QH, CW), BF16),
            pltpu.VMEM((NCH, 2, QT, CW), BF16),
            pltpu.VMEM((NCH, QT, CW), BF16),
            dma(5), dma(NCH),
            dma(NZ, 2), dma(NZ, 2),
            dma(NZ, 6), dma(NZ, 6),
            dma(9, NX), dma(9, NX),
            dma(NZ, NX), dma(NZ, NX),
            dma(NP), dma(NP), dma(NZ), dma(NZ), dma(NZ), dma(NZ), dma(NP), dma(NP),
            dma(NCH, 4), dma(NCH, 4),
        ],
        compiler_params=pltpu.CompilerParams(
            collective_id=0, has_side_effects=True, vmem_limit_bytes=60 * 1024 * 1024
        ),
    )(queries, key_rows, values, gate_input, norm_gain, out_weight.T)
    return pl.pallas_call(
        land,
        out_shape=jax.ShapeDtypeStruct((QT, D), BF16),
        in_specs=[anyspec],
        out_specs=anyspec,
        scratch_shapes=[pltpu.VMEM((QT, D), BF16), dma(2, 8)],
    )(out)


def solution(mesh):
    in_specs = (
        P("seq", "head"),
        P("seq", "head"),
        P("seq", "head"),
        P("seq", "head"),
        P("head"),
        P("head", "seq"),
    )
    return jax.shard_map(
        per_device,
        mesh=mesh,
        in_specs=in_specs,
        out_specs=P(("seq", "head"), None),
        check_vma=False,
    )
```
